32 devices in a mesh: groups: 2 (over x), lon: 16 (over z, y, core).
Axes of the slice: x: 2, y: 2, z: 4, core: 2. Of those that a mesh axis runs over, the one named last changes fastest.
Arguments:
- latlon_fields: bfloat16 [32, 32, 2048], P('groups', 'lon'), parts along dimension 0, may hold values from -6 to 6
- remap_table: int32 [2, 32, 2048], P(None, None, 'lon'), may hold values from 0 to 2047, as said below
- kernel_first: bfloat16 [3, 3, 64, 16], replicated, may hold values from -0.5 to 0.5
- kernel_second: bfloat16 [3, 3, 64, 64], replicated, may hold values from -0.25 to 0.25
- kernel_down: bfloat16 [3, 3, 128, 64], replicated, may hold values from -0.25 to 0.25
- kernel_coarse: bfloat16 [3, 3, 128, 128], replicated, may hold values from -0.1875 to 0.1875
- kernel_up: bfloat16 [3, 3, 64, 128], replicated, may hold values from -0.375 to 0.375
- kernel_merge: bfloat16 [3, 3, 64, 128], replicated, may hold values from -0.1875 to 0.1875
- projection: bfloat16 [8, 64], replicated, may hold values from -0.75 to 0.75
Outputs:
- forecast: float32 [16, 32, 2048], P('groups', None, 'lon'), parts along dimension 0
The draws below stay inside these ranges and needn't reach their ends.
There are 2 independent parts, one for each index of `groups`. The reference program is written for one: setup_inputs(seed, part) draws one part's arguments, and reference() takes and returns one part's arrays. A program takes and returns all parts, laid end to end along the dimension named above; an argument that names none is the same for every part. Nothing has to cross between parts.
Inputs may be any that keep to these rules, and one draw needn't show every extreme that they name: remap_table[0] is a lat-lon row below 32; remap_table[1] is a lat-lon column, and for a grid cell in column w it lies in the same block of 128 columns as w, that is between (w // 128) * 128 and (w // 128) * 128 + 127.
All inputs are finite; a program needn't handle non-finite values.
Results may differ from the reference program's by a relative error of at most 0.00084.
Values may be sent and summed in bfloat16 or wider, within the bound.
A program may use at most 128 MiB of HBM per device.

```python
import jax
import jax.numpy as jnp
from jax import lax

C = 64
C2 = 128
CIN = 16
COUT = 8
H = 32
WD = 128
W = 2048
NLAT = 32


def draw_remap_table(key, part):
    key_rows, key_cols = jax.random.split(jax.random.fold_in(key, 7))
    row_index = jnp.broadcast_to(jnp.arange(H, dtype=jnp.int32)[:, None], (H, W))
    col_index = jnp.broadcast_to(jnp.arange(W, dtype=jnp.int32)[None, :], (H, W))
    jitter_rows = jax.random.randint(key_rows, (H, W), -2, 3, dtype=jnp.int32)
    latitude = jnp.clip(row_index * NLAT // H + jitter_rows, 0, NLAT - 1)
    owners = col_index // WD
    offset = col_index % WD
    jitter_cols = jax.random.randint(key_cols, (H, W), -1, 2, dtype=jnp.int32)
    longitude = owners * WD + jnp.clip(offset + jitter_cols, 0, WD - 1)
    latitude = latitude.at[0, 0].set(0)
    longitude = longitude.at[0, 0].set(0)
    longitude = longitude.at[H - 1, W - 1].set(W - 1)
    return jnp.stack([latitude, longitude]).astype(jnp.int32)


def steps_of(own_key, dims, cuts, least, largest):
    def one(axis_at, blocks):
        steps = jax.random.uniform(jax.random.fold_in(jax.random.fold_in(own_key, 6), axis_at), (blocks,), jnp.float32, least / len(cuts), largest / len(cuts))
        return jnp.repeat(jnp.exp(steps), dims[axis_at] // blocks).reshape((-1,) + (1,) * (len(dims) - axis_at - 1))

    level = one(*cuts[0])
    for cut in cuts[1:]:
        level = level * one(*cut)
    return level


def noise(stream_key, dims, width, most, shards=(), kind=jnp.bfloat16):
    entries = jax.random.normal(stream_key, dims, jnp.float32) * width
    if len(shards) > 0:
        entries = steps_of(stream_key, dims, shards, -0.22, 0.18) * entries
    return jnp.clip(entries, min=-most, max=most).astype(kind)


def setup_inputs(seed: int = 0, part: int = 0) -> dict:
    splits = jax.random.split(jax.random.key(seed), 10)
    part_keys = jax.random.split(jax.random.fold_in(splits[9], part), 10)
    return {
        "latlon_fields": noise(part_keys[0], (CIN, NLAT, W), 1.0, 6.0, ((1, 16),)),
        "remap_table": draw_remap_table(jax.random.fold_in(splits[9], 71), part),
        "kernel_first": noise(splits[2], (3, 3, C, CIN), (9 * CIN) ** -0.5, 0.5),
        "kernel_second": noise(splits[3], (3, 3, C, C), (9 * C) ** -0.5, 0.25),
        "kernel_down": noise(splits[4], (3, 3, C2, C), (9 * C) ** -0.5, 0.25),
        "kernel_coarse": noise(splits[5], (3, 3, C2, C2), (9 * C2) ** -0.5, 0.1875),
        "kernel_up": noise(splits[6], (3, 3, C, C2), (9 * C2 // 4) ** -0.5, 0.375),
        "kernel_merge": noise(splits[7], (3, 3, C, 2 * C), (18 * C) ** -0.5, 0.1875),
        "projection": noise(splits[8], (COUT, C), C ** -0.5, 0.75),
    }


def extend_full(field_in):
    half = field_in.shape[2] // 2
    top_row = jnp.roll(field_in[:, :1], half, axis=2)
    bottom_row = jnp.zeros_like(field_in[:, :1])
    tall = jnp.concatenate([top_row, field_in, bottom_row], axis=1)
    return jnp.concatenate([tall[:, :, -1:], tall, tall[:, :, :1]], axis=2)


def convolve(extended, kernel, stride):
    channels = extended.shape[0]
    out_rows = (extended.shape[1] - 2) // stride
    out_cols = (extended.shape[2] - 2) // stride
    source = extended.astype(jnp.float32)
    weights = kernel.astype(jnp.float32)
    total = jnp.zeros((kernel.shape[2], out_rows, out_cols), jnp.float32)
    for row_tap in range(3):
        for col_tap in range(3):
            piece = lax.slice(source, (0, row_tap, col_tap),
                              (channels, row_tap + (out_rows - 1) * stride + 1, col_tap + (out_cols - 1) * stride + 1),
                              (1, stride, stride))
            total = total + jnp.einsum("oc,chw->ohw", weights[row_tap, col_tap], piece,
                                       precision=lax.Precision.HIGHEST)
    return total


def activate(values):
    return jax.nn.silu(values).astype(jnp.bfloat16)


def reference(latlon_fields, remap_table, kernel_first, kernel_second, kernel_down, kernel_coarse, kernel_up, kernel_merge, projection):
    remapped = latlon_fields[:, remap_table[0], remap_table[1]]
    first = activate(convolve(extend_full(remapped), kernel_first, 1))
    second = activate(convolve(extend_full(first), kernel_second, 1))
    coarse_in = activate(convolve(extend_full(second), kernel_down, 2))
    coarse_out = activate(convolve(extend_full(coarse_in), kernel_coarse, 1))
    grid_rows = second.shape[1]
    grid_cols = second.shape[2]
    stuffed = jnp.zeros((coarse_out.shape[0], grid_rows, grid_cols), jnp.float32)
    stuffed = stuffed.at[:, ::2, ::2].set(coarse_out.astype(jnp.float32))
    padded = jnp.pad(stuffed, ((0, 0), (1, 1), (0, 0)))
    padded = jnp.concatenate([padded[:, :, -1:], padded, padded[:, :, :1]], axis=2)
    lifted = convolve(padded, kernel_up, 1)
    upsampled = activate(lifted)
    joined = jnp.concatenate([second, upsampled], axis=0)
    merged = activate(convolve(extend_full(joined), kernel_merge, 1))
    count_out = projection.shape[0]
    update = jnp.einsum("oc,chw->ohw", projection.astype(jnp.float32), merged.astype(jnp.float32),
                        precision=lax.Precision.HIGHEST)
    return remapped[:count_out].astype(jnp.float32) + update
```

```python
import functools

import jax
import jax.numpy as jnp
from jax import lax
from jax.experimental import pallas as pl
from jax.experimental.pallas import tpu as pltpu
from jax.sharding import PartitionSpec as P

MESH = pl.DeviceIdType.MESH
F32 = jnp.float32
BF16 = jnp.bfloat16
HALO = 8
PER = 8
OFFSETS = (0, 1, 2, -1)
NT = (((1,), (1,)), ((), ()))


def dot_nt(a, b):
    return lax.dot_general(a, b, NT, preferred_element_type=F32)


def silu(x):
    half = 0.5 * x
    return half * jnp.tanh(half) + half


def dot_nn(a, b):
    return jnp.dot(a, b, preferred_element_type=F32)


def clear(*arrays):
    for w in arrays:
        w[...] = jnp.zeros_like(w)


def fill(w, kernel, cin, first_in):
    C = kernel.shape[2]
    for q in range(2):
        for p in range(2):
            for a in range(4):
                for l, off in enumerate(OFFSETS):
                    kr, kcol = a - q, off - p + 1
                    if 0 <= kr < 3 and 0 <= kcol < 3:
                        at = (q * 2 + p) * C
                        lane = a * 4 * cin + l * cin
                        w[at : at + C, lane : lane + cin] = kernel[kr, kcol][:, first_in : first_in + cin]


def fine_weights(k1, k2, km, w1, wlast, wfirst, wnext, w2, wma, wmb):
    channels, C = k1.shape[2], k1.shape[3]
    wide = PER * channels
    clear(w1, wlast, wfirst, wnext, w2, wma, wmb)
    for p in range(2):
        for l, off in enumerate(OFFSETS):
            if not 0 <= off - p + 1 < 3:
                continue
            k = [k1[kr, off - p + 1] for kr in range(3)]
            lane = l * wide
            for r in range(PER):
                at = (r * 2 + p) * C
                for kr in range(3):
                    if 0 <= r + kr - 1 < PER:
                        to = lane + (r + kr - 1) * channels
                        w1[to : to + channels, at : at + C] = k[kr]
            end = lane + (PER - 1) * channels
            wlast[end : end + channels, p * C : (p + 1) * C] = k[0]
            wfirst[lane : lane + channels, p * C : (p + 1) * C] = k[0]
            wnext[lane : lane + channels, p * C : (p + 1) * C] = k[2]
    fill(w2, k2, C, 0)
    fill(wma, km, C, 0)
    fill(wmb, km, C, C)


def coarse_weights(kd, kc, ku, kp, wd, wc, wu, wp):
    C, C2 = kd.shape[2], kd.shape[3]
    COUT = kp.shape[0]
    clear(wd, wc, wu, wp)
    for a in range(3):
        for l, kcol in ((0, 1), (1, 2), (3, 0)):
            wd[a * 4 * C + l * C : a * 4 * C + (l + 1) * C] = kd[a, kcol]
        for s, kcol in enumerate((1, 2, 0)):
            wc[:, (a * 3 + s) * C2 : (a * 3 + s + 1) * C2] = kc[a, kcol]
    for q, rows in ((0, ((0, 1),)), (1, ((0, 0), (1, 2)))):
        for p, columns in ((0, ((0, 1),)), (1, ((0, 0), (1, 2)))):
            at = (q * 2 + p) * C
            for ri, kr in rows:
                for ci, kcol in columns:
                    lane = (ri * 2 + ci) * C2
                    wu[at : at + C, lane : lane + C2] = ku[kr, kcol]
    for g in range(4):
        wp[g * COUT : (g + 1) * COUT, g * C : (g + 1) * C] = kp[...].astype(F32)


def exchange_kernel(n, lat_ref, tab_hbm, k1_hbm, k2_hbm, kd_hbm, kc_hbm, ku_hbm, km_hbm, kp_hbm,
                    own_ref, left_ref, right_ref, anti_ref, anti_left_ref, anti_right_ref,
                    w1, wlast, wfirst, wnext, w2, wd, wc, wu, wma, wmb, wp,
                    tab_ref, k1, k2, kd, kc, ku, km, kp, recv, edge, hot, send_sem, recv_sem, own_sem, hsend, hrecv, load_sem):
    me = lax.axis_index("lon")
    group = lax.axis_index("groups")
    cols = recv.shape[3]
    height = tab_ref.shape[1]
    per = height // own_ref.shape[0]
    sub_rows = lat_ref.shape[1]
    channels = own_ref.shape[2] // per
    barrier = pltpu.get_barrier_semaphore()

    def greet(d, carry):
        pl.semaphore_signal(barrier, inc=1, device_id=(group, lax.rem(me + d, n)), device_id_type=MESH)
        return carry

    lax.fori_loop(1, n, greet, 0)
    mine = pltpu.make_async_copy(lat_ref.at[:, :, pl.ds(pl.multiple_of(me * cols, cols), cols)], recv.at[me], own_sem)
    mine.start()
    loads = [pltpu.make_async_copy(src, dst, load_sem.at[i]) for i, (src, dst) in enumerate((
        (tab_hbm, tab_ref), (k1_hbm, k1), (k2_hbm, k2), (kd_hbm, kd), (kc_hbm, kc), (ku_hbm, ku), (km_hbm, km), (kp_hbm, kp)))]
    for load in loads:
        load.start()
    pl.semaphore_wait(barrier, n - 1)

    def block_copy(d, slot):
        target = lax.rem(me + d, n)
        return pltpu.make_async_remote_copy(
            src_ref=lat_ref.at[:, :, pl.ds(pl.multiple_of(target * cols, cols), cols)],
            dst_ref=recv.at[slot],
            send_sem=send_sem.at[d - 1],
            recv_sem=recv_sem.at[d - 1],
            device_id=(group, target),
            device_id_type=MESH,
        )

    def send(d, carry):
        block_copy(d, me).start()
        return carry

    lax.fori_loop(1, n, send, 0)

    loads[0].wait()
    p = lax.broadcasted_iota(jnp.int32, (cols, cols), 0)
    w = lax.broadcasted_iota(jnp.int32, (cols, cols), 1)
    half = cols // 2
    perm = (w == jnp.where(p < half, 2 * p, 2 * p - cols + 1)).astype(F32).astype(BF16)
    rows_at = dot_nt(perm, tab_ref[0].astype(F32).astype(BF16)).astype(jnp.int32)
    cols_at = dot_nt(perm, (tab_ref[1] - me * cols).astype(F32).astype(BF16)).astype(jnp.int32)
    wide = per * channels
    lane = lax.broadcasted_iota(jnp.int32, (cols, wide), 1)
    wide_hot = lax.broadcasted_iota(jnp.int32, (cols, 2 * cols), 1)
    held = sub_rows * channels
    per_tile = wide // held
    spot = lane // held * sub_rows + lane % sub_rows
    pair = rows_at // (2 * sub_rows)
    col_key = cols_at + rows_at // sub_rows % 2 * cols
    row_key = pair * sub_rows + rows_at % sub_rows
    for h in range(height):
        hot[h * cols : (h + 1) * cols] = (col_key[:, h : h + 1] == wide_hot).astype(F32).astype(BF16)
    at_row = [jnp.broadcast_to(row_key[:, h : h + 1], (cols, wide)) - spot for h in range(height)]
    fi = lax.broadcasted_iota(jnp.int32, (per * wide, wide), 0)
    fo = lax.broadcasted_iota(jnp.int32, (per * wide, wide), 1)
    fold = ((fi // wide == fo // channels) & (fi % held // sub_rows == fo % channels)).astype(F32).astype(BF16)
    for load in loads[1:]:
        load.wait()
    coarse_weights(kd, kc, ku, kp, wd, wc, wu, wp)
    fine_weights(k1, k2, km, w1, wlast, wfirst, wnext, w2, wma, wmb)

    mine.wait()

    def receive(d, carry):
        block_copy(d, lax.rem(me - d + n, n)).wait_recv()
        return carry

    lax.fori_loop(1, n, receive, 0)

    def halo(k, src, dst, shift):
        return pltpu.make_async_remote_copy(
            src_ref=src, dst_ref=dst, send_sem=hsend.at[k], recv_sem=hrecv.at[k],
            device_id=(group, lax.rem(me + shift + 2 * n, n)), device_id_type=MESH)

    copies = [
        halo(0, own_ref.at[0], anti_ref, n // 2),
        halo(1, edge.at[1, 0], anti_left_ref, n // 2 + 1),
        halo(2, edge.at[0, 0], anti_right_ref, n // 2 - 1),
        halo(3, edge.at[1], left_ref, 1),
        halo(4, edge.at[0], right_ref, -1),
    ]
    arrived = recv[...].reshape(n // 2, 2, held, cols)
    source = jnp.concatenate([arrived[:, 0], arrived[:, 1]], axis=2).reshape(n // 2 * held, 2 * cols)
    tiles = source.shape[0] // wide
    for g in range(own_ref.shape[0]):
        got = dot_nt(hot[g * per * cols : (g + 1) * per * cols], source)
        picked = []
        for q in range(per):
            one = jnp.zeros((cols, wide), F32)
            for t in range(tiles):
                value = got[q * cols : (q + 1) * cols, t * wide : (t + 1) * wide]
                one = jnp.where(at_row[g * per + q] == t * per_tile * sub_rows, value, one)
            picked.append(one.astype(BF16))
        block = jnp.dot(jnp.concatenate(picked, axis=1), fold, preferred_element_type=F32)
        own_ref[g] = block.astype(BF16)
        edge[0, g] = jnp.concatenate([block[0:HALO], block[half : half + HALO]], axis=0).astype(BF16)
        edge[1, g] = jnp.concatenate([block[half - HALO : half], block[cols - HALO : cols]], axis=0).astype(BF16)
        if g == 0:
            for c in copies[:3]:
                c.start()

    for c in copies[3:]:
        c.start()

    def sent(d, carry):
        block_copy(d, me).wait_send()
        return carry

    lax.fori_loop(1, n, sent, 0)
    for c in copies:
        c.wait()


def unet_kernel(own_ref, left_ref, right_ref, anti_ref, anti_left_ref, anti_right_ref,
                w1, wlast, wfirst, wnext, w2, wd, wc, wu, wma, wmb, wp, out_ref, xf, x1, x2, x3, xc, xu):
    groups, cols, wide = own_ref.shape
    height = groups * PER
    channels = wide // PER
    half = cols // 2
    J = half + 2 * HALO
    C = w2.shape[0] // 4
    C2 = wd.shape[1]
    COUT = wp.shape[0] // 4
    pairs = height // 2
    AB = pairs + 1

    def spread(g, l, r):
        even = jnp.concatenate([g[:half], r[:HALO], l[:HALO]], axis=0)
        odd = jnp.concatenate([g[half:], r[HALO:], l[HALO:]], axis=0)
        return jnp.concatenate([even, odd, pltpu.roll(even, J - 1, 0), pltpu.roll(odd, 1, 0)], axis=1).astype(BF16)

    for g in range(groups):
        xf[g] = spread(own_ref[g].astype(F32), left_ref[g].astype(F32), right_ref[g].astype(F32))
    xf[groups] = spread(anti_ref[...].astype(F32), anti_left_ref[...].astype(F32), anti_right_ref[...].astype(F32))

    def neighbours(v):
        count = v.shape[0]
        v = v.reshape(count // J, J, v.shape[1])
        lane = lax.broadcasted_iota(jnp.int32, v.shape, 2)
        other = jnp.where(lane < C, pltpu.roll(v, J - 1, 1), pltpu.roll(v, 1, 1))
        return jnp.concatenate([v, other], axis=2).astype(BF16)

    def store_pair(x, i0, count, s):
        x[pl.ds(i0, count), 1] = neighbours(s[:, : 2 * C])
        x[pl.ds(i0 + 1, count), 0] = neighbours(s[:, 2 * C :])

    def wrap(x):
        x[0, 0] = x[AB, 1]
        x[AB, 0] = x[0, 1]
        x[AB - 1, 1] = jnp.zeros(x.shape[2:], BF16)

    def taps(x, i0, count, a, width):
        v = x[pl.ds(i0 + a // 2, count), a % 2, 0:width]
        return v.reshape(count * width, v.shape[-1])

    B = pairs

    def own_loop(steps, body):
        for t in range(steps):
            body(t)

    every = groups + 1
    acc = dot_nn(xf[...].reshape(every * J, 4 * wide), w1[...]).reshape(every, J, PER * 2 * C)
    from_last = dot_nn(xf[pl.ds(0, groups - 1)].reshape((groups - 1) * J, 4 * wide), wlast[...]).reshape(groups - 1, J, 2 * C)
    from_next = dot_nn(xf[pl.ds(1, groups - 1)].reshape((groups - 1) * J, 4 * wide), wnext[...]).reshape(groups - 1, J, 2 * C)
    own_top = dot_nn(xf[groups], wfirst[...])
    anti_top = dot_nn(xf[0], wfirst[...])
    for g in range(every):
        for r in range(PER):
            v = acc[g, :, r * 2 * C : (r + 1) * 2 * C]
            if r == 0:
                v = v + (anti_top if g == groups else own_top if g == 0 else from_last[g - 1])
            if r == PER - 1 and g < groups - 1:
                v = v + from_next[g]
            slot = g * PER + r + 1 + (2 if g == groups else 0)
            if slot // 2 < x1.shape[0]:
                x1[slot // 2, slot % 2] = neighbours(silu(v))[0]
    wrap(x1)

    def second(i0, count):
        acc = dot_nt(taps(x1, i0, count, 0, J), w2[:, : 4 * C])
        for a in range(1, 4):
            acc += dot_nt(taps(x1, i0, count, a, J), w2[:, a * 4 * C : (a + 1) * 4 * C])
        store_pair(x2, i0, count, silu(acc))

    second(AB, 2)
    own_loop(pairs // B, lambda t: second(t * B, B))
    wrap(x2)

    def shifts(v, both):
        v = v.reshape(v.shape[0] // J, J, v.shape[1])
        parts = [v, pltpu.roll(v, J - 1, 1)]
        if both:
            parts.append(pltpu.roll(v, 1, 1))
        return jnp.concatenate(parts, axis=2).astype(BF16)

    def down(i0, slot, count):
        acc = dot_nn(taps(x2, i0, count, 0, J), wd[: 4 * C])
        for a in range(1, 3):
            acc += dot_nn(taps(x2, i0, count, a, J), wd[a * 4 * C : (a + 1) * 4 * C])
        xc[pl.ds(slot, count)] = shifts(silu(acc), True)

    down(AB, pairs + 3, 2)
    own_loop(pairs // B, lambda t: down(t * B, t * B + 1, B))
    xc[0] = xc[pairs + 3]
    xc[pairs + 2] = xc[1]
    xc[pairs + 1] = jnp.zeros(xc.shape[1:], BF16)

    def coarse(i0, slot, count):
        acc = None
        for a in range(3):
            v = xc[pl.ds(i0 + a, count)].reshape(count * J, 3 * C2)
            part = dot_nt(v, wc[:, a * 3 * C2 : (a + 1) * 3 * C2])
            acc = part if acc is None else acc + part
        xu[pl.ds(slot, count)] = shifts(silu(acc), False)

    coarse(pairs + 2, pairs + 1, 1)
    own_loop(pairs // B, lambda t: coarse(t * B, t * B, B))
    xu[pairs] = jnp.zeros(xu.shape[1:], BF16)

    def up(i0, count):
        acc = dot_nt(xu[pl.ds(i0, count)].reshape(count * J, 2 * C2), wu[:, : 2 * C2])
        return silu(acc + dot_nt(xu[pl.ds(i0 + 1, count)].reshape(count * J, 2 * C2), wu[:, 2 * C2 :]))

    def up_own(t):
        store_pair(x3, t * B, B, up(t * B, B))

    own_loop(pairs // B, up_own)
    v = xu[pairs + 1]
    x3[0, 0] = neighbours(silu(dot_nt(v, wu[0 : 2 * C, : 2 * C2])))[0]
    x3[AB - 1, 1] = jnp.zeros(x3.shape[2:], BF16)

    p = lax.broadcasted_iota(jnp.int32, (cols, cols), 0)
    w = lax.broadcasted_iota(jnp.int32, (cols, cols), 1)
    unperm = (w == jnp.where(p < half, 2 * p, 2 * p - cols + 1)).astype(F32)
    wpb = wp[...].astype(BF16)

    for t in range(pairs // B):
        i0 = t * B
        acc = None
        for a in range(4):
            for x, w in ((x2, wma), (x3, wmb)):
                part = dot_nt(taps(x, i0, B, a, half), w[:, a * 4 * C : (a + 1) * 4 * C])
                acc = part if acc is None else acc + part
        merged = silu(acc).astype(BF16)
        update = dot_nt(wpb, merged)
        lines = []
        plain = [own_ref[g].astype(F32).T for g in range(groups)]
        for b in range(B):
            u = update[:, b * half : (b + 1) * half]
            for q in range(2):
                line = jnp.concatenate([u[2 * q * COUT : (2 * q + 1) * COUT], u[(2 * q + 1) * COUT : (2 * q + 2) * COUT]], axis=1)
                h = 2 * (i0 + b) + q
                at = (h % PER) * channels
                lines.append(line + plain[h // PER][at : at + COUT])
        woven = jnp.dot(jnp.concatenate(lines, axis=0), unperm, precision=lax.Precision.HIGHEST, preferred_element_type=F32)
        for m in range(2 * B):
            out_ref[:, 2 * i0 + m, :] = woven[m * COUT : (m + 1) * COUT]


def shards(latlon, table, k1, k2, kd, kc, ku, km, kp):
    n = lax.axis_size("lon")
    k1, kd = jnp.swapaxes(k1, 2, 3), jnp.swapaxes(kd, 2, 3)
    channels, sub_rows, width = latlon.shape
    height, cols = table.shape[1], table.shape[2]
    vm = pl.BlockSpec(memory_space=pltpu.VMEM)
    groups = height // PER
    edges = jax.ShapeDtypeStruct((groups, 2 * HALO, PER * channels), BF16)
    corner = jax.ShapeDtypeStruct((2 * HALO, PER * channels), BF16)
    C, C2, COUT = k1.shape[3], kd.shape[3], kp.shape[0]
    weights = (
        jax.ShapeDtypeStruct((4 * PER * channels, 2 * C * PER), BF16),
        jax.ShapeDtypeStruct((4 * PER * channels, 2 * C), BF16),
        jax.ShapeDtypeStruct((4 * PER * channels, 2 * C), BF16),
        jax.ShapeDtypeStruct((4 * PER * channels, 2 * C), BF16),
        jax.ShapeDtypeStruct((4 * C, 16 * C), BF16),
        jax.ShapeDtypeStruct((12 * C, C2), BF16),
        jax.ShapeDtypeStruct((C2, 9 * C2), BF16),
        jax.ShapeDtypeStruct((4 * C, 4 * C2), BF16),
        jax.ShapeDtypeStruct((4 * C, 16 * C), BF16),
        jax.ShapeDtypeStruct((4 * C, 16 * C), BF16),
        jax.ShapeDtypeStruct((4 * COUT, 4 * C), F32),
    )
    ready = pl.pallas_call(
        functools.partial(exchange_kernel, n),
        out_shape=(jax.ShapeDtypeStruct((groups, cols, PER * channels), BF16), edges, edges,
                   jax.ShapeDtypeStruct((cols, PER * channels), BF16), corner, corner) + weights,
        in_specs=[pl.BlockSpec(memory_space=pltpu.HBM)] * 9,
        out_specs=(vm,) * 17,
        scratch_shapes=[
            pltpu.VMEM(table.shape, table.dtype),
        ] + [pltpu.VMEM(k.shape, BF16) for k in (k1, k2, kd, kc, ku, km, kp)] + [
            pltpu.VMEM((n, channels, sub_rows, cols), BF16),
            pltpu.VMEM((2, groups, 2 * HALO, PER * channels), BF16),
            pltpu.VMEM((height * cols, 2 * cols), BF16),
            pltpu.SemaphoreType.DMA((n - 1,)),
            pltpu.SemaphoreType.DMA((n - 1,)),
            pltpu.SemaphoreType.DMA,
            pltpu.SemaphoreType.DMA((5,)),
            pltpu.SemaphoreType.DMA((5,)),
            pltpu.SemaphoreType.DMA((8,)),
        ],
        compiler_params=pltpu.CompilerParams(collective_id=0, has_side_effects=True, vmem_limit_bytes=32 * 2**20),
        name="exchange",
    )(*(pltpu.with_memory_space_constraint(v, pltpu.HBM) for v in (latlon, table, k1, k2, kd, kc, ku, km, kp)))
    J = cols // 2 + 2 * HALO
    pairs = height // 2
    return pl.pallas_call(
        unet_kernel,
        out_shape=jax.ShapeDtypeStruct((COUT, height, cols), F32),
        in_specs=[vm] * 17,
        out_specs=vm,
        scratch_shapes=[
            pltpu.VMEM((height // PER + 1, J, 4 * PER * channels), BF16),
            pltpu.VMEM((pairs + 5, 2, J, 4 * C), BF16),
            pltpu.VMEM((pairs + 4, 2, J, 4 * C), BF16),
            pltpu.VMEM((pairs + 1, 2, J, 4 * C), BF16),
            pltpu.VMEM((pairs + 5, J, 3 * C2), BF16),
            pltpu.VMEM((pairs + 2, J, 2 * C2), BF16),
        ],
        compiler_params=pltpu.CompilerParams(vmem_limit_bytes=32 * 2**20),
        name="unet",
    )(*ready)


def solution(mesh):
    return jax.shard_map(
        shards,
        mesh=mesh,
        in_specs=(P("groups", "lon", None), P(None, None, "lon")) + (P(),) * 7,
        out_specs=P("groups", None, "lon"),
        check_vma=False,
    )
```

```python
import functools

import jax
import jax.numpy as jnp
from jax import lax
from jax.experimental import pallas as pl
from jax.experimental.pallas import tpu as pltpu
from jax.sharding import PartitionSpec as P

MESH = pl.DeviceIdType.MESH
F32 = jnp.float32
BF16 = jnp.bfloat16
HALO = 4
PER = 8
OFFSETS = (0, 1, 2, -1)
NT = (((1,), (1,)), ((), ()))


def dot_nt(a, b):
    return lax.dot_general(a, b, NT, preferred_element_type=F32)


def silu(x):
    half = 0.5 * x
    return half * jnp.tanh(half) + half


def dot_nn(a, b):
    return jnp.dot(a, b, preferred_element_type=F32)


def clear(*arrays):
    for w in arrays:
        w[...] = jnp.zeros_like(w)


def fill(w, kernel, cin, first_in):
    C = kernel.shape[2]
    for q in range(2):
        for p in range(2):
            for a in range(4):
                for l, off in enumerate(OFFSETS):
                    kr, kcol = a - q, off - p + 1
                    if 0 <= kr < 3 and 0 <= kcol < 3:
                        at = (q * 2 + p) * C
                        lane = a * 4 * cin + l * cin
                        w[at : at + C, lane : lane + cin] = kernel[kr, kcol][:, first_in : first_in + cin]


def fine_weights(k1, k2, km, w1, wlast, wfirst, wnext, w2, wma, wmb):
    channels, C = k1.shape[2], k1.shape[3]
    wide = PER * channels
    clear(w1, wlast, wfirst, wnext, w2, wma, wmb)
    for p in range(2):
        for l, off in enumerate(OFFSETS):
            if not 0 <= off - p + 1 < 3:
                continue
            k = [k1[kr, off - p + 1] for kr in range(3)]
            lane = l * wide
            for r in range(PER):
                at = (r * 2 + p) * C
                for kr in range(3):
                    if 0 <= r + kr - 1 < PER:
                        to = lane + (r + kr - 1) * channels
                        w1[to : to + channels, at : at + C] = k[kr]
            end = lane + (PER - 1) * channels
            wlast[end : end + channels, p * C : (p + 1) * C] = k[0]
            wfirst[lane : lane + channels, p * C : (p + 1) * C] = k[0]
            wnext[lane : lane + channels, p * C : (p + 1) * C] = k[2]
    fill(w2, k2, C, 0)
    fill(wma, km, C, 0)
    fill(wmb, km, C, C)


def coarse_weights(kd, kc, ku, kp, wd, wc, wu, wp):
    C, C2 = kd.shape[2], kd.shape[3]
    COUT = kp.shape[0]
    clear(wd, wc, wu, wp)
    for a in range(3):
        for l, kcol in ((0, 1), (1, 2), (3, 0)):
            wd[a * 4 * C + l * C : a * 4 * C + (l + 1) * C] = kd[a, kcol]
        for s, kcol in enumerate((1, 2, 0)):
            wc[:, (a * 3 + s) * C2 : (a * 3 + s + 1) * C2] = kc[a, kcol]
    for q, rows in ((0, ((0, 1),)), (1, ((0, 0), (1, 2)))):
        for p, columns in ((0, ((0, 1),)), (1, ((0, 0), (1, 2)))):
            at = (q * 2 + p) * C
            for ri, kr in rows:
                for ci, kcol in columns:
                    lane = (ri * 2 + ci) * C2
                    wu[at : at + C, lane : lane + C2] = ku[kr, kcol]
    for g in range(4):
        wp[g * COUT : (g + 1) * COUT, g * C : (g + 1) * C] = kp[...].astype(F32)


def exchange_kernel(n, lat_ref, tab_hbm, k1_hbm, k2_hbm, kd_hbm, kc_hbm, ku_hbm, km_hbm, kp_hbm,
                    own_ref, halo_ref, w1, wlast, wfirst, wnext, w2, wd, wc, wu, wma, wmb, wp,
                    tab_ref, k1, k2, kd, kc, ku, km, kp, recv, edge, hot, edge_hot,
                    send_sem, recv_sem, own_sem, hsend, hrecv, load_sem):
    me = lax.axis_index("lon")
    group = lax.axis_index("groups")
    cols = recv.shape[3]
    height = tab_ref.shape[1]
    per = height // own_ref.shape[0]
    sub_rows = lat_ref.shape[1]
    channels = own_ref.shape[2] // per
    barrier = pltpu.get_barrier_semaphore()

    def greet(d, carry):
        pl.semaphore_signal(barrier, inc=1, device_id=(group, lax.rem(me + d, n)), device_id_type=MESH)
        return carry

    lax.fori_loop(1, n, greet, 0)
    mine = pltpu.make_async_copy(lat_ref.at[:, :, pl.ds(pl.multiple_of(me * cols, cols), cols)], recv.at[me], own_sem)
    mine.start()
    loads = [pltpu.make_async_copy(src, dst, load_sem.at[i]) for i, (src, dst) in enumerate((
        (tab_hbm, tab_ref), (k1_hbm, k1), (k2_hbm, k2), (kd_hbm, kd), (kc_hbm, kc), (ku_hbm, ku), (km_hbm, km), (kp_hbm, kp)))]
    for load in loads:
        load.start()
    pl.semaphore_wait(barrier, n - 1)

    def block_copy(d, slot):
        target = lax.rem(me + d, n)
        return pltpu.make_async_remote_copy(
            src_ref=lat_ref.at[:, :, pl.ds(pl.multiple_of(target * cols, cols), cols)],
            dst_ref=recv.at[slot],
            send_sem=send_sem,
            recv_sem=recv_sem,
            device_id=(group, target),
            device_id_type=MESH,
        )

    def send(d, carry):
        block_copy(d, me).start()
        return carry

    lax.fori_loop(1, n, send, 0)

    loads[0].wait()
    p = lax.broadcasted_iota(jnp.int32, (cols, cols), 0)
    w = lax.broadcasted_iota(jnp.int32, (cols, cols), 1)
    half = cols // 2
    perm = (w == jnp.where(p < half, 2 * p, 2 * p - cols + 1)).astype(F32).astype(BF16)
    rows_at = dot_nt(perm, tab_ref[0].astype(F32).astype(BF16)).astype(jnp.int32)
    cols_at = dot_nt(perm, (tab_ref[1] - me * cols).astype(F32).astype(BF16)).astype(jnp.int32)
    wide = per * channels
    lane = lax.broadcasted_iota(jnp.int32, (cols, wide), 1)
    wide_hot = lax.broadcasted_iota(jnp.int32, (cols, 2 * cols), 1)
    held = sub_rows * channels
    per_tile = wide // held
    spot = lane // held * sub_rows + lane % sub_rows
    pair = rows_at // (2 * sub_rows)
    col_key = cols_at + rows_at // sub_rows % 2 * cols
    row_key = pair * sub_rows + rows_at % sub_rows
    groups = own_ref.shape[0]
    strip = 2 * HALO
    ep = lax.broadcasted_iota(jnp.int32, (2 * strip, cols), 0)
    ew = lax.broadcasted_iota(jnp.int32, (2 * strip, cols), 1)
    first = jnp.where(ep < HALO, 2 * ep, 2 * (ep - HALO) + 1)
    last = jnp.where(ep < strip + HALO, 2 * (ep - strip) + 1, 2 * (ep - strip - HALO)) + cols - strip
    edge_perm = (ew == jnp.where(ep < strip, first, last)).astype(F32).astype(BF16)
    edge_rows = dot_nt(edge_perm, tab_ref[0].astype(F32).astype(BF16)).astype(jnp.int32)
    edge_cols = dot_nt(edge_perm, (tab_ref[1] - me * cols).astype(F32).astype(BF16)).astype(jnp.int32)
    edge_col_key = edge_cols + edge_rows // sub_rows % 2 * cols
    edge_row_key = edge_rows // (2 * sub_rows) * sub_rows + edge_rows % sub_rows
    edge_held = 2 * groups * strip

    def edge_of(keys, q, width):
        return jnp.concatenate([jnp.broadcast_to(keys[side * strip : (side + 1) * strip, g * per + q : g * per + q + 1], (strip, width))
                                for side in range(2) for g in range(groups)], axis=0)

    for q in range(per):
        edge_hot[q * edge_held : (q + 1) * edge_held] = (edge_of(edge_col_key, q, 2 * cols) == wide_hot[:edge_held]).astype(F32).astype(BF16)
    edge_at = [edge_of(edge_row_key, q, wide) - spot[:edge_held] for q in range(per)]
    for h in range(height):
        hot[h * cols : (h + 1) * cols] = (col_key[:, h : h + 1] == wide_hot).astype(F32).astype(BF16)
    at_row = [jnp.broadcast_to(row_key[:, h : h + 1], (cols, wide)) - spot for h in range(height)]
    fi = lax.broadcasted_iota(jnp.int32, (per * wide, wide), 0)
    fo = lax.broadcasted_iota(jnp.int32, (per * wide, wide), 1)
    fold = ((fi // wide == fo // channels) & (fi % held // sub_rows == fo % channels)).astype(F32).astype(BF16)
    for load in loads[1:]:
        load.wait()
    coarse_weights(kd, kc, ku, kp, wd, wc, wu, wp)
    fine_weights(k1, k2, km, w1, wlast, wfirst, wnext, w2, wma, wmb)

    mine.wait()

    blocks = pltpu.make_async_remote_copy(
        src_ref=recv.at[pl.ds(0, n - 1)], dst_ref=recv.at[pl.ds(0, n - 1)], send_sem=send_sem, recv_sem=recv_sem,
        device_id=(group, lax.rem(me + 1, n)), device_id_type=MESH)
    blocks.wait_recv()

    def halo(src, dst, shift):
        return pltpu.make_async_remote_copy(
            src_ref=src, dst_ref=dst, send_sem=hsend, recv_sem=hrecv,
            device_id=(group, lax.rem(me + shift + 2 * n, n)), device_id_type=MESH)

    lead = groups * strip
    firsts, lasts = edge.at[pl.ds(0, lead)], edge.at[pl.ds(lead, lead)]
    arrived = recv[...].reshape(n // 2, 2, held, cols)
    source = jnp.concatenate([arrived[:, 0], arrived[:, 1]], axis=2).reshape(n // 2 * held, 2 * cols)
    tiles = source.shape[0] // wide

    def pick(got, at, q, count):
        one = jnp.zeros((count, wide), F32)
        for t in range(tiles):
            value = got[q * count : (q + 1) * count, t * wide : (t + 1) * wide]
            one = jnp.where(at == t * per_tile * sub_rows, value, one)
        return one.astype(BF16)

    got = dot_nt(edge_hot[...], source)
    picked = [pick(got, edge_at[q], q, edge_held) for q in range(per)]
    edge[...] = jnp.dot(jnp.concatenate(picked, axis=1), fold, preferred_element_type=F32).astype(BF16)
    for src, first_row, count, shift in (
        (lasts, cols + 4 * strip, lead, 1), (firsts, cols + 4 * strip + lead, lead, -1),
        (edge.at[pl.ds(lead, 2 * strip)], cols, 2 * strip, n // 2 + 1), (edge.at[pl.ds(0, 2 * strip)], cols + 2 * strip, 2 * strip, n // 2 - 1),
    ):
        halo(src, halo_ref.at[pl.ds(first_row, count)], shift).start()
    for g in range(groups):
        got = dot_nt(hot[g * per * cols : (g + 1) * per * cols], source)
        picked = [pick(got, at_row[g * per + q], q, cols) for q in range(per)]
        own_ref[g] = jnp.dot(jnp.concatenate(picked, axis=1), fold, preferred_element_type=F32).astype(BF16)
        if g == 0:
            halo(own_ref.at[0], halo_ref.at[pl.ds(0, cols)], n // 2).start()

    blocks.wait_send()
    every = halo(halo_ref, halo_ref, 1)
    every.wait_send()
    every.wait_recv()


def unet_kernel(own_ref, halo_ref, w1, wlast, wfirst, wnext, w2, wd, wc, wu, wma, wmb, wp, out_ref, xf, x1, x2, x3, xc, xu):
    groups, cols, wide = own_ref.shape
    height = groups * PER
    channels = wide // PER
    half = cols // 2
    J = half + 2 * HALO
    C = w2.shape[0] // 4
    C2 = wd.shape[1]
    COUT = wp.shape[0] // 4
    pairs = height // 2
    AB = pairs + 1

    strip = 2 * HALO
    upper = lax.broadcasted_iota(jnp.int32, (strip, wide), 0) < HALO

    def spread(g, l, r):
        even = jnp.concatenate([g[:half], jnp.where(upper, r, l)], axis=0)
        odd = jnp.concatenate([g[half:], pltpu.roll(jnp.where(upper, l, r), HALO, 0)], axis=0)
        return jnp.concatenate([even, odd, pltpu.roll(even, J - 1, 0), pltpu.roll(odd, 1, 0)], axis=1).astype(BF16)

    around = halo_ref[...].astype(F32)
    corners, sides = around[cols : cols + 4 * strip], around[cols + 4 * strip :]
    for g in range(groups):
        xf[g] = spread(own_ref[g].astype(F32), sides[g * strip : (g + 1) * strip], sides[(groups + g) * strip : (groups + g + 1) * strip])
    xf[groups] = spread(around[:cols], corners[:strip], corners[2 * strip : 3 * strip])

    def neighbours(v):
        count = v.shape[0]
        v = v.reshape(count // J, J, v.shape[1])
        lane = lax.broadcasted_iota(jnp.int32, v.shape, 2)
        other = jnp.where(lane < C, pltpu.roll(v, J - 1, 1), pltpu.roll(v, 1, 1))
        return jnp.concatenate([v, other], axis=2).astype(BF16)

    def store_pair(x, i0, count, s):
        x[pl.ds(i0, count), 1] = neighbours(s[:, : 2 * C])
        x[pl.ds(i0 + 1, count), 0] = neighbours(s[:, 2 * C :])

    def wrap(x):
        x[0, 0] = x[AB, 1]
        x[AB, 0] = x[0, 1]
        x[AB - 1, 1] = jnp.zeros(x.shape[2:], BF16)

    def taps(x, i0, count, a, width):
        v = x[pl.ds(i0 + a // 2, count), a % 2, 0:width]
        return v.reshape(count * width, v.shape[-1])

    B = 8
    BM = 4

    def own_loop(steps, body):
        for t in range(steps):
            body(t)

    every = groups + 1
    acc = dot_nn(xf[...].reshape(every * J, 4 * wide), w1[...]).reshape(every, J, PER * 2 * C)
    from_last = dot_nn(xf[pl.ds(0, groups - 1)].reshape((groups - 1) * J, 4 * wide), wlast[...]).reshape(groups - 1, J, 2 * C)
    from_next = dot_nn(xf[pl.ds(1, groups - 1)].reshape((groups - 1) * J, 4 * wide), wnext[...]).reshape(groups - 1, J, 2 * C)
    own_top = dot_nn(xf[groups], wfirst[...])
    anti_top = dot_nn(xf[0], wfirst[...])
    for g in range(every):
        for r in range(PER):
            v = acc[g, :, r * 2 * C : (r + 1) * 2 * C]
            if r == 0:
                v = v + (anti_top if g == groups else own_top if g == 0 else from_last[g - 1])
            if r == PER - 1 and g < groups - 1:
                v = v + from_next[g]
            slot = g * PER + r + 1 + (2 if g == groups else 0)
            if slot // 2 < x1.shape[0]:
                x1[slot // 2, slot % 2] = neighbours(silu(v))[0]
    wrap(x1)

    def second(i0, count):
        acc = dot_nt(jnp.concatenate([taps(x1, i0, count, a, J) for a in range(4)], axis=1), w2[...])
        store_pair(x2, i0, count, silu(acc))

    second(AB, 2)
    own_loop(pairs // B, lambda t: second(t * B, B))
    wrap(x2)

    def shifts(v, both):
        v = v.reshape(v.shape[0] // J, J, v.shape[1])
        parts = [v, pltpu.roll(v, J - 1, 1)]
        if both:
            parts.append(pltpu.roll(v, 1, 1))
        return jnp.concatenate(parts, axis=2).astype(BF16)

    def down(i0, slot, count):
        acc = dot_nn(jnp.concatenate([taps(x2, i0, count, a, J) for a in range(3)], axis=1), wd[...])
        xc[pl.ds(slot, count)] = shifts(silu(acc), True)

    down(AB, pairs + 3, 2)
    own_loop(pairs // B, lambda t: down(t * B, t * B + 1, B))
    xc[0] = xc[pairs + 3]
    xc[pairs + 2] = xc[1]
    xc[pairs + 1] = jnp.zeros(xc.shape[1:], BF16)

    def coarse(i0, slot, count):
        acc = dot_nt(jnp.concatenate([xc[pl.ds(i0 + a, count)].reshape(count * J, 3 * C2) for a in range(3)], axis=1), wc[...])
        xu[pl.ds(slot, count)] = shifts(silu(acc), False)

    coarse(pairs + 2, pairs + 1, 1)
    own_loop(pairs // B, lambda t: coarse(t * B, t * B, B))
    xu[pairs] = jnp.zeros(xu.shape[1:], BF16)

    def up(i0, count):
        return silu(dot_nt(jnp.concatenate([xu[pl.ds(i0 + a, count)].reshape(count * J, 2 * C2) for a in range(2)], axis=1), wu[...]))

    def up_own(t):
        store_pair(x3, t * B, B, up(t * B, B))

    own_loop(pairs // B, up_own)
    v = xu[pairs + 1]
    x3[0, 0] = neighbours(silu(dot_nt(v, wu[0 : 2 * C, : 2 * C2])))[0]
    x3[AB - 1, 1] = jnp.zeros(x3.shape[2:], BF16)

    p = lax.broadcasted_iota(jnp.int32, (cols, cols), 0)
    w = lax.broadcasted_iota(jnp.int32, (cols, cols), 1)
    unperm = (w == jnp.where(p < half, 2 * p, 2 * p - cols + 1)).astype(F32).astype(BF16)
    unperm = jnp.concatenate([unperm, unperm], axis=0)
    wpb = wp[...].astype(BF16)
    plain = [own_ref[g].astype(F32).T for g in range(groups)]

    def merge(i0, count):
        tiles = [taps(x, i0, count, a, half) for x in (x2, x3) for a in range(4)]
        return silu(dot_nt(jnp.concatenate(tiles, axis=1), jnp.concatenate([wma[...], wmb[...]], axis=1))).astype(BF16)

    merged = [merge(t * BM, BM) for t in range(pairs // BM)]
    lines = []
    for t in range(pairs // BM):
        update = dot_nt(wpb, merged[t])
        for b in range(BM):
            u = update[:, b * half : (b + 1) * half]
            for q in range(2):
                line = jnp.concatenate([u[2 * q * COUT : (2 * q + 1) * COUT], u[(2 * q + 1) * COUT : (2 * q + 2) * COUT]], axis=1)
                h = 2 * (t * BM + b) + q
                at = (h % PER) * channels
                lines.append(line + plain[h // PER][at : at + COUT])
    lines = jnp.concatenate(lines, axis=0)
    high = lines.astype(BF16)
    low = (lines - high.astype(F32)).astype(BF16)
    woven = dot_nn(jnp.concatenate([high, low], axis=1), unperm)
    for h in range(height):
        out_ref[:, h, :] = woven[h * COUT : (h + 1) * COUT]


def shards(latlon, table, k1, k2, kd, kc, ku, km, kp):
    n = lax.axis_size("lon")
    k1, kd = jnp.swapaxes(k1, 2, 3), jnp.swapaxes(kd, 2, 3)
    channels, sub_rows, width = latlon.shape
    height, cols = table.shape[1], table.shape[2]
    vm = pl.BlockSpec(memory_space=pltpu.VMEM)
    groups = height // PER
    sides = 2 * groups * 2 * HALO
    around = jax.ShapeDtypeStruct((cols + 8 * HALO + sides, PER * channels), BF16)
    C, C2, COUT = k1.shape[3], kd.shape[3], kp.shape[0]
    weights = (
        jax.ShapeDtypeStruct((4 * PER * channels, 2 * C * PER), BF16),
        jax.ShapeDtypeStruct((4 * PER * channels, 2 * C), BF16),
        jax.ShapeDtypeStruct((4 * PER * channels, 2 * C), BF16),
        jax.ShapeDtypeStruct((4 * PER * channels, 2 * C), BF16),
        jax.ShapeDtypeStruct((4 * C, 16 * C), BF16),
        jax.ShapeDtypeStruct((12 * C, C2), BF16),
        jax.ShapeDtypeStruct((C2, 9 * C2), BF16),
        jax.ShapeDtypeStruct((4 * C, 4 * C2), BF16),
        jax.ShapeDtypeStruct((4 * C, 16 * C), BF16),
        jax.ShapeDtypeStruct((4 * C, 16 * C), BF16),
        jax.ShapeDtypeStruct((4 * COUT, 4 * C), F32),
    )
    ready = pl.pallas_call(
        functools.partial(exchange_kernel, n),
        out_shape=(jax.ShapeDtypeStruct((groups, cols, PER * channels), BF16), around) + weights,
        in_specs=[pl.BlockSpec(memory_space=pltpu.HBM)] * 9,
        out_specs=(vm,) * 13,
        scratch_shapes=[
            pltpu.VMEM(table.shape, table.dtype),
        ] + [pltpu.VMEM(k.shape, BF16) for k in (k1, k2, kd, kc, ku, km, kp)] + [
            pltpu.VMEM((n, channels, sub_rows, cols), BF16),
            pltpu.VMEM((sides, PER * channels), BF16),
            pltpu.VMEM((height * cols, 2 * cols), BF16),
            pltpu.VMEM((PER * sides, 2 * cols), BF16),
            pltpu.SemaphoreType.DMA,
            pltpu.SemaphoreType.DMA,
            pltpu.SemaphoreType.DMA,
            pltpu.SemaphoreType.DMA,
            pltpu.SemaphoreType.DMA,
            pltpu.SemaphoreType.DMA((8,)),
        ],
        compiler_params=pltpu.CompilerParams(collective_id=0, has_side_effects=True, vmem_limit_bytes=32 * 2**20),
        name="exchange",
    )(*(pltpu.with_memory_space_constraint(v, pltpu.HBM) for v in (latlon, table, k1, k2, kd, kc, ku, km, kp)))
    J = cols // 2 + 2 * HALO
    pairs = height // 2
    return pl.pallas_call(
        unet_kernel,
        out_shape=jax.ShapeDtypeStruct((COUT, height, cols), F32),
        in_specs=[vm] * 13,
        out_specs=vm,
        scratch_shapes=[
            pltpu.VMEM((height // PER + 1, J, 4 * PER * channels), BF16),
            pltpu.VMEM((pairs + 5, 2, J, 4 * C), BF16),
            pltpu.VMEM((pairs + 4, 2, J, 4 * C), BF16),
            pltpu.VMEM((pairs + 1, 2, J, 4 * C), BF16),
            pltpu.VMEM((pairs + 5, J, 3 * C2), BF16),
            pltpu.VMEM((pairs + 2, J, 2 * C2), BF16),
        ],
        compiler_params=pltpu.CompilerParams(vmem_limit_bytes=32 * 2**20),
        name="unet",
    )(*ready)


def solution(mesh):
    return jax.shard_map(
        shards,
        mesh=mesh,
        in_specs=(P("groups", "lon", None), P(None, None, "lon")) + (P(),) * 7,
        out_specs=P("groups", None, "lon"),
        check_vma=False,
    )
```

```python
import functools

import jax
import jax.numpy as jnp
from jax import lax
from jax.experimental import pallas as pl
from jax.experimental.pallas import tpu as pltpu
from jax.sharding import PartitionSpec as P

MESH = pl.DeviceIdType.MESH
F32 = jnp.float32
BF16 = jnp.bfloat16
HALO = 4
PER = 8
OFFSETS = (0, 1, 2, -1)
NT = (((1,), (1,)), ((), ()))


def dot_nt(a, b):
    return lax.dot_general(a, b, NT, preferred_element_type=F32)


def silu(x):
    half = 0.5 * x
    return half * jnp.tanh(half) + half


def dot_nn(a, b):
    return jnp.dot(a, b, preferred_element_type=F32)


def clear(*arrays):
    for w in arrays:
        w[...] = jnp.zeros_like(w)


def fill(w, kernel, cin, first_in):
    C = kernel.shape[2]
    for q in range(2):
        for p in range(2):
            for a in range(4):
                for l, off in enumerate(OFFSETS):
                    kr, kcol = a - q, off - p + 1
                    if 0 <= kr < 3 and 0 <= kcol < 3:
                        at = (q * 2 + p) * C
                        lane = a * 4 * cin + l * cin
                        w[at : at + C, lane : lane + cin] = kernel[kr, kcol][:, first_in : first_in + cin]


def fine_weights(k1, k2, km, w1, wlast, wfirst, wnext, w2, wma, wmb):
    channels, C = k1.shape[2], k1.shape[3]
    wide = PER * channels
    clear(w1, wlast, wfirst, wnext, w2, wma, wmb)
    for p in range(2):
        for l, off in enumerate(OFFSETS):
            if not 0 <= off - p + 1 < 3:
                continue
            k = [k1[kr, off - p + 1] for kr in range(3)]
            lane = l * wide
            for r in range(PER):
                at = (r * 2 + p) * C
                for kr in range(3):
                    if 0 <= r + kr - 1 < PER:
                        to = lane + (r + kr - 1) * channels
                        w1[to : to + channels, at : at + C] = k[kr]
            end = lane + (PER - 1) * channels
            wlast[end : end + channels, p * C : (p + 1) * C] = k[0]
            wfirst[lane : lane + channels, p * C : (p + 1) * C] = k[0]
            wnext[lane : lane + channels, p * C : (p + 1) * C] = k[2]
    fill(w2, k2, C, 0)
    fill(wma, km, C, 0)
    fill(wmb, km, C, C)


def coarse_weights(kd, kc, ku, kp, wd, wc, wu, wp):
    C, C2 = kd.shape[2], kd.shape[3]
    COUT = kp.shape[0]
    clear(wd, wc, wu, wp)
    for a in range(3):
        for l, kcol in ((0, 1), (1, 2), (3, 0)):
            wd[a * 4 * C + l * C : a * 4 * C + (l + 1) * C] = kd[a, kcol]
        for s, kcol in enumerate((1, 2, 0)):
            wc[:, (a * 3 + s) * C2 : (a * 3 + s + 1) * C2] = kc[a, kcol]
    for q, rows in ((0, ((0, 1),)), (1, ((0, 0), (1, 2)))):
        for p, columns in ((0, ((0, 1),)), (1, ((0, 0), (1, 2)))):
            at = (q * 2 + p) * C
            for ri, kr in rows:
                for ci, kcol in columns:
                    lane = (ri * 2 + ci) * C2
                    wu[at : at + C, lane : lane + C2] = ku[kr, kcol]
    for g in range(4):
        wp[g * COUT : (g + 1) * COUT, g * C : (g + 1) * C] = kp[...].astype(F32)


def exchange_kernel(n, lat_ref, tab_hbm, k1_hbm, k2_hbm, kd_hbm, kc_hbm, ku_hbm, km_hbm, kp_hbm,
                    own_ref, halo_ref, w1, wlast, wfirst, wnext, w2, wd, wc, wu, wma, wmb, wp,
                    tab_ref, k1, k2, kd, kc, ku, km, kp, recv, edge, hot, edge_hot, edge_at, at_ref, fold_ref,
                    send_sem, recv_sem, own_sem, hsend, hrecv, load_sem):
    me = lax.axis_index("lon")
    group = lax.axis_index("groups")
    cols = recv.shape[3]
    height = tab_ref.shape[1]
    per = height // own_ref.shape[0]
    sub_rows = lat_ref.shape[1]
    channels = own_ref.shape[2] // per
    barrier = pltpu.get_barrier_semaphore()

    def greet(d, carry):
        pl.semaphore_signal(barrier, inc=1, device_id=(group, lax.rem(me + d, n)), device_id_type=MESH)
        return carry

    lax.fori_loop(1, n, greet, 0)
    mine = pltpu.make_async_copy(lat_ref.at[:, :, pl.ds(pl.multiple_of(me * cols, cols), cols)], recv.at[me], own_sem)
    mine.start()
    loads = [pltpu.make_async_copy(src, dst, load_sem.at[i]) for i, (src, dst) in enumerate((
        (tab_hbm, tab_ref), (k1_hbm, k1), (k2_hbm, k2), (kd_hbm, kd), (kc_hbm, kc), (ku_hbm, ku), (km_hbm, km), (kp_hbm, kp)))]
    for load in loads:
        load.start()
    pl.semaphore_wait(barrier, n - 1)

    def block_copy(target):
        return pltpu.make_async_remote_copy(
            src_ref=lat_ref.at[:, :, pl.ds(pl.multiple_of(target * cols, cols), cols)],
            dst_ref=recv.at[me],
            send_sem=send_sem,
            recv_sem=recv_sem,
            device_id=(group, target),
            device_id_type=MESH,
        )

    def send(k, carry):
        target = n - 4 - k // 4 * 4 + (me + k + 1) % 4

        @pl.when(target != me)
        def _():
            block_copy(target).start()

        return carry

    lax.fori_loop(0, n, send, 0)

    loads[0].wait()
    p = lax.broadcasted_iota(jnp.int32, (cols, cols), 0)
    w = lax.broadcasted_iota(jnp.int32, (cols, cols), 1)
    half = cols // 2
    perm = (w == jnp.where(p < half, 2 * p, 2 * p - cols + 1)).astype(F32).astype(BF16)
    rows_at = dot_nt(perm, tab_ref[0].astype(F32).astype(BF16)).astype(jnp.int32)
    cols_at = dot_nt(perm, (tab_ref[1] - me * cols).astype(F32).astype(BF16)).astype(jnp.int32)
    wide = per * channels
    lane = lax.broadcasted_iota(jnp.int32, (cols, wide), 1)
    wide_hot = lax.broadcasted_iota(jnp.int32, (cols, 2 * cols), 1)
    held = sub_rows * channels
    per_tile = wide // held
    spot = lane // held * sub_rows + lane % sub_rows
    pair = rows_at // (2 * sub_rows)
    col_key = cols_at + rows_at // sub_rows % 2 * cols
    row_key = pair * sub_rows + rows_at % sub_rows
    groups = own_ref.shape[0]
    strip = 2 * HALO
    ep = lax.broadcasted_iota(jnp.int32, (2 * strip, cols), 0)
    ew = lax.broadcasted_iota(jnp.int32, (2 * strip, cols), 1)
    first = jnp.where(ep < HALO, 2 * ep, 2 * (ep - HALO) + 1)
    last = jnp.where(ep < strip + HALO, 2 * (ep - strip) + 1, 2 * (ep - strip - HALO)) + cols - strip
    edge_perm = (ew == jnp.where(ep < strip, first, last)).astype(F32).astype(BF16)
    edge_rows = dot_nt(edge_perm, tab_ref[0].astype(F32).astype(BF16)).astype(jnp.int32)
    edge_cols = dot_nt(edge_perm, (tab_ref[1] - me * cols).astype(F32).astype(BF16)).astype(jnp.int32)
    edge_col_key = edge_cols + edge_rows // sub_rows % 2 * cols
    edge_row_key = edge_rows // (2 * sub_rows) * sub_rows + edge_rows % sub_rows
    edge_held = 2 * groups * strip

    def edge_of(keys, q, width):
        return jnp.concatenate([jnp.broadcast_to(keys[side * strip : (side + 1) * strip, g * per + q : g * per + q + 1], (strip, width))
                                for side in range(2) for g in range(groups)], axis=0)

    for q in range(per):
        edge_hot[q * edge_held : (q + 1) * edge_held] = (edge_of(edge_col_key, q, 2 * cols) == wide_hot[:edge_held]).astype(F32).astype(BF16)
        edge_at[q * edge_held : (q + 1) * edge_held] = edge_of(edge_row_key, q, wide) - spot[:edge_held]
    for h in range(height):
        hot[h * cols : (h + 1) * cols] = (col_key[:, h : h + 1] == wide_hot).astype(F32).astype(BF16)
        at_ref[h * cols : (h + 1) * cols] = jnp.broadcast_to(row_key[:, h : h + 1], (cols, wide)) - spot
    fi = lax.broadcasted_iota(jnp.int32, (per * wide, wide), 0)
    fo = lax.broadcasted_iota(jnp.int32, (per * wide, wide), 1)
    fold_ref[...] = ((fi // wide == fo // channels) & (fi % held // sub_rows == fo % channels)).astype(F32).astype(BF16)
    mine.wait()

    blocks = pltpu.make_async_remote_copy(
        src_ref=recv.at[pl.ds(0, n - 1)], dst_ref=recv.at[pl.ds(0, n - 1)], send_sem=send_sem, recv_sem=recv_sem,
        device_id=(group, lax.rem(me + 1, n)), device_id_type=MESH)
    blocks.wait_recv()

    def halo(src, dst, shift):
        return pltpu.make_async_remote_copy(
            src_ref=src, dst_ref=dst, send_sem=hsend, recv_sem=hrecv,
            device_id=(group, lax.rem(me + shift + 2 * n, n)), device_id_type=MESH)

    lead = groups * strip
    firsts, lasts = edge.at[pl.ds(0, lead)], edge.at[pl.ds(lead, lead)]

    def source_of():
        arrived = recv[...].reshape(n // 2, 2, held, cols)
        return jnp.concatenate([arrived[:, 0], arrived[:, 1]], axis=2).reshape(n // 2 * held, 2 * cols)

    tiles = n // 2 * held // wide

    def pick(got, at, q, count):
        one = jnp.zeros((count, wide), F32)
        for t in range(tiles):
            value = got[q * count : (q + 1) * count, t * wide : (t + 1) * wide]
            one = jnp.where(at == t * per_tile * sub_rows, value, one)
        return one.astype(BF16)

    got = dot_nt(edge_hot[...], source_of())
    picked = [pick(got, edge_at[q * edge_held : (q + 1) * edge_held], q, edge_held) for q in range(per)]
    edge[...] = jnp.dot(jnp.concatenate(picked, axis=1), fold_ref[...], preferred_element_type=F32).astype(BF16)
    for src, first_row, count, shift in (
        (lasts, cols + 4 * strip, lead, 1), (firsts, cols + 4 * strip + lead, lead, -1),
        (edge.at[pl.ds(lead, 2 * strip)], cols, 2 * strip, n // 2 + 1), (edge.at[pl.ds(0, 2 * strip)], cols + 2 * strip, 2 * strip, n // 2 - 1),
    ):
        halo(src, halo_ref.at[pl.ds(first_row, count)], shift).start()

    @pl.when(me >= 0)
    def _():
        source = source_of()
        for g in range(groups):
            got = dot_nt(hot[g * per * cols : (g + 1) * per * cols], source)
            picked = [pick(got, at_ref[(g * per + q) * cols : (g * per + q + 1) * cols], q, cols) for q in range(per)]
            own_ref[g] = jnp.dot(jnp.concatenate(picked, axis=1), fold_ref[...], preferred_element_type=F32).astype(BF16)
            if g == 0:
                halo(own_ref.at[0], halo_ref.at[pl.ds(0, cols)], n // 2).start()

    for load in loads[1:]:
        load.wait()
    coarse_weights(kd, kc, ku, kp, wd, wc, wu, wp)
    fine_weights(k1, k2, km, w1, wlast, wfirst, wnext, w2, wma, wmb)
    blocks.wait_send()
    every = halo(halo_ref, halo_ref, 1)
    every.wait_send()
    every.wait_recv()


def unet_kernel(own_ref, halo_ref, w1, wlast, wfirst, wnext, w2, wd, wc, wu, wma, wmb, wp, out_ref, xf, x1, x2, x3, xc, xu):
    groups, cols, wide = own_ref.shape
    height = groups * PER
    channels = wide // PER
    half = cols // 2
    J = half + 2 * HALO
    C = w2.shape[0] // 4
    C2 = wd.shape[1]
    COUT = wp.shape[0] // 4
    pairs = height // 2
    AB = pairs + 1

    strip = 2 * HALO
    upper = lax.broadcasted_iota(jnp.int32, (strip, wide), 0) < HALO

    def spread(g, l, r):
        even = jnp.concatenate([g[:half], jnp.where(upper, r, l)], axis=0)
        odd = jnp.concatenate([g[half:], pltpu.roll(jnp.where(upper, l, r), HALO, 0)], axis=0)
        return jnp.concatenate([even, odd, pltpu.roll(even, J - 1, 0), pltpu.roll(odd, 1, 0)], axis=1).astype(BF16)

    around = halo_ref[...].astype(F32)
    corners, sides = around[cols : cols + 4 * strip], around[cols + 4 * strip :]
    for g in range(groups):
        xf[g] = spread(own_ref[g].astype(F32), sides[g * strip : (g + 1) * strip], sides[(groups + g) * strip : (groups + g + 1) * strip])
    xf[groups] = spread(around[:cols], corners[:strip], corners[2 * strip : 3 * strip])

    def neighbours(v):
        count = v.shape[0]
        v = v.reshape(count // J, J, v.shape[1])
        lane = lax.broadcasted_iota(jnp.int32, v.shape, 2)
        other = jnp.where(lane < C, pltpu.roll(v, J - 1, 1), pltpu.roll(v, 1, 1))
        return jnp.concatenate([v, other], axis=2).astype(BF16)

    def store_pair(x, i0, count, s):
        x[pl.ds(i0, count), 1] = neighbours(s[:, : 2 * C])
        x[pl.ds(i0 + 1, count), 0] = neighbours(s[:, 2 * C :])

    def wrap(x):
        x[0, 0] = x[AB, 1]
        x[AB, 0] = x[0, 1]
        x[AB - 1, 1] = jnp.zeros(x.shape[2:], BF16)

    def taps(x, i0, count, a, width):
        v = x[pl.ds(i0 + a // 2, count), a % 2, 0:width]
        return v.reshape(count * width, v.shape[-1])

    B = 8
    BM = 4

    def own_loop(steps, body):
        for t in range(steps):
            body(t)

    every = groups + 1
    acc = dot_nn(xf[...].reshape(every * J, 4 * wide), w1[...]).reshape(every, J, PER * 2 * C)
    from_last = dot_nn(xf[pl.ds(0, groups - 1)].reshape((groups - 1) * J, 4 * wide), wlast[...]).reshape(groups - 1, J, 2 * C)
    from_next = dot_nn(xf[pl.ds(1, groups - 1)].reshape((groups - 1) * J, 4 * wide), wnext[...]).reshape(groups - 1, J, 2 * C)
    own_top = dot_nn(xf[groups], wfirst[...])
    anti_top = dot_nn(xf[0], wfirst[...])
    for g in range(every):
        for r in range(PER):
            v = acc[g, :, r * 2 * C : (r + 1) * 2 * C]
            if r == 0:
                v = v + (anti_top if g == groups else own_top if g == 0 else from_last[g - 1])
            if r == PER - 1 and g < groups - 1:
                v = v + from_next[g]
            slot = g * PER + r + 1 + (2 if g == groups else 0)
            if slot // 2 < x1.shape[0]:
                x1[slot // 2, slot % 2] = neighbours(silu(v))[0]
    wrap(x1)

    def second(i0, count):
        acc = dot_nt(jnp.concatenate([taps(x1, i0, count, a, J) for a in range(4)], axis=1), w2[...])
        store_pair(x2, i0, count, silu(acc))

    second(AB, 2)
    own_loop(pairs // B, lambda t: second(t * B, B))
    wrap(x2)

    def shifts(v, both):
        v = v.reshape(v.shape[0] // J, J, v.shape[1])
        parts = [v, pltpu.roll(v, J - 1, 1)]
        if both:
            parts.append(pltpu.roll(v, 1, 1))
        return jnp.concatenate(parts, axis=2).astype(BF16)

    def down(i0, slot, count):
        acc = dot_nn(jnp.concatenate([taps(x2, i0, count, a, J) for a in range(3)], axis=1), wd[...])
        xc[pl.ds(slot, count)] = shifts(silu(acc), True)

    down(AB, pairs + 3, 2)
    own_loop(pairs // B, lambda t: down(t * B, t * B + 1, B))
    xc[0] = xc[pairs + 3]
    xc[pairs + 2] = xc[1]
    xc[pairs + 1] = jnp.zeros(xc.shape[1:], BF16)

    def coarse(i0, slot, count):
        acc = dot_nt(jnp.concatenate([xc[pl.ds(i0 + a, count)].reshape(count * J, 3 * C2) for a in range(3)], axis=1), wc[...])
        xu[pl.ds(slot, count)] = shifts(silu(acc), False)

    coarse(pairs + 2, pairs + 1, 1)
    own_loop(pairs // B, lambda t: coarse(t * B, t * B, B))
    xu[pairs] = jnp.zeros(xu.shape[1:], BF16)

    def up(i0, count):
        return silu(dot_nt(jnp.concatenate([xu[pl.ds(i0 + a, count)].reshape(count * J, 2 * C2) for a in range(2)], axis=1), wu[...]))

    def up_own(t):
        store_pair(x3, t * B, B, up(t * B, B))

    own_loop(pairs // B, up_own)
    v = xu[pairs + 1]
    x3[0, 0] = neighbours(silu(dot_nt(v, wu[0 : 2 * C, : 2 * C2])))[0]
    x3[AB - 1, 1] = jnp.zeros(x3.shape[2:], BF16)

    p = lax.broadcasted_iota(jnp.int32, (cols, cols), 0)
    w = lax.broadcasted_iota(jnp.int32, (cols, cols), 1)
    unperm = (w == jnp.where(p < half, 2 * p, 2 * p - cols + 1)).astype(F32).astype(BF16)
    unperm = jnp.concatenate([unperm, unperm], axis=0)
    wpb = wp[...].astype(BF16)
    plain = [own_ref[g].astype(F32).T for g in range(groups)]

    def merge(i0, count):
        tiles = [taps(x, i0, count, a, half) for x in (x2, x3) for a in range(4)]
        return silu(dot_nt(jnp.concatenate(tiles, axis=1), jnp.concatenate([wma[...], wmb[...]], axis=1))).astype(BF16)

    merged = [merge(t * BM, BM) for t in range(pairs // BM)]
    lines = []
    for t in range(pairs // BM):
        update = dot_nt(wpb, merged[t])
        for b in range(BM):
            u = update[:, b * half : (b + 1) * half]
            for q in range(2):
                line = jnp.concatenate([u[2 * q * COUT : (2 * q + 1) * COUT], u[(2 * q + 1) * COUT : (2 * q + 2) * COUT]], axis=1)
                h = 2 * (t * BM + b) + q
                at = (h % PER) * channels
                lines.append(line + plain[h // PER][at : at + COUT])
    lines = jnp.concatenate(lines, axis=0)
    high = lines.astype(BF16)
    low = (lines - high.astype(F32)).astype(BF16)
    woven = dot_nn(jnp.concatenate([high, low], axis=1), unperm)
    for h in range(height):
        out_ref[:, h, :] = woven[h * COUT : (h + 1) * COUT]


def shards(latlon, table, k1, k2, kd, kc, ku, km, kp):
    n = lax.axis_size("lon")
    k1, kd = jnp.swapaxes(k1, 2, 3), jnp.swapaxes(kd, 2, 3)
    channels, sub_rows, width = latlon.shape
    height, cols = table.shape[1], table.shape[2]
    vm = pl.BlockSpec(memory_space=pltpu.VMEM)
    groups = height // PER
    sides = 2 * groups * 2 * HALO
    around = jax.ShapeDtypeStruct((cols + 8 * HALO + sides, PER * channels), BF16)
    C, C2, COUT = k1.shape[3], kd.shape[3], kp.shape[0]
    weights = (
        jax.ShapeDtypeStruct((4 * PER * channels, 2 * C * PER), BF16),
        jax.ShapeDtypeStruct((4 * PER * channels, 2 * C), BF16),
        jax.ShapeDtypeStruct((4 * PER * channels, 2 * C), BF16),
        jax.ShapeDtypeStruct((4 * PER * channels, 2 * C), BF16),
        jax.ShapeDtypeStruct((4 * C, 16 * C), BF16),
        jax.ShapeDtypeStruct((12 * C, C2), BF16),
        jax.ShapeDtypeStruct((C2, 9 * C2), BF16),
        jax.ShapeDtypeStruct((4 * C, 4 * C2), BF16),
        jax.ShapeDtypeStruct((4 * C, 16 * C), BF16),
        jax.ShapeDtypeStruct((4 * C, 16 * C), BF16),
        jax.ShapeDtypeStruct((4 * COUT, 4 * C), F32),
    )
    ready = pl.pallas_call(
        functools.partial(exchange_kernel, n),
        out_shape=(jax.ShapeDtypeStruct((groups, cols, PER * channels), BF16), around) + weights,
        in_specs=[pl.BlockSpec(memory_space=pltpu.HBM)] * 9,
        out_specs=(vm,) * 13,
        scratch_shapes=[
            pltpu.VMEM(table.shape, table.dtype),
        ] + [pltpu.VMEM(k.shape, BF16) for k in (k1, k2, kd, kc, ku, km, kp)] + [
            pltpu.VMEM((n, channels, sub_rows, cols), BF16),
            pltpu.VMEM((sides, PER * channels), BF16),
            pltpu.VMEM((height * cols, 2 * cols), BF16),
            pltpu.VMEM((PER * sides, 2 * cols), BF16),
            pltpu.VMEM((PER * sides, PER * channels), jnp.int32),
            pltpu.VMEM((height * cols, PER * channels), jnp.int32),
            pltpu.VMEM((PER * PER * channels, PER * channels), BF16),
            pltpu.SemaphoreType.DMA,
            pltpu.SemaphoreType.DMA,
            pltpu.SemaphoreType.DMA,
            pltpu.SemaphoreType.DMA,
            pltpu.SemaphoreType.DMA,
            pltpu.SemaphoreType.DMA((8,)),
        ],
        compiler_params=pltpu.CompilerParams(collective_id=0, has_side_effects=True, vmem_limit_bytes=32 * 2**20),
        name="exchange",
    )(*(pltpu.with_memory_space_constraint(v, pltpu.HBM) for v in (latlon, table, k1, k2, kd, kc, ku, km, kp)))
    J = cols // 2 + 2 * HALO
    pairs = height // 2
    return pl.pallas_call(
        unet_kernel,
        out_shape=jax.ShapeDtypeStruct((COUT, height, cols), F32),
        in_specs=[vm] * 13,
        out_specs=vm,
        scratch_shapes=[
            pltpu.VMEM((height // PER + 1, J, 4 * PER * channels), BF16),
            pltpu.VMEM((pairs + 5, 2, J, 4 * C), BF16),
            pltpu.VMEM((pairs + 4, 2, J, 4 * C), BF16),
            pltpu.VMEM((pairs + 1, 2, J, 4 * C), BF16),
            pltpu.VMEM((pairs + 5, J, 3 * C2), BF16),
            pltpu.VMEM((pairs + 2, J, 2 * C2), BF16),
        ],
        compiler_params=pltpu.CompilerParams(vmem_limit_bytes=32 * 2**20),
        name="unet",
    )(*ready)


def solution(mesh):
    return jax.shard_map(
        shards,
        mesh=mesh,
        in_specs=(P("groups", "lon", None), P(None, None, "lon")) + (P(),) * 7,
        out_specs=P("groups", None, "lon"),
        check_vma=False,
    )
```

```python
import functools

import jax
import jax.numpy as jnp
from jax import lax
from jax.experimental import pallas as pl
from jax.experimental.pallas import tpu as pltpu
from jax.sharding import PartitionSpec as P

MESH = pl.DeviceIdType.MESH
F32 = jnp.float32
BF16 = jnp.bfloat16
HALO = 4
PER = 8
OFFSETS = (0, 1, 2, -1)
NT = (((1,), (1,)), ((), ()))


def dot_nt(a, b):
    return lax.dot_general(a, b, NT, preferred_element_type=F32)


def silu(x):
    half = 0.5 * x
    return half * jnp.tanh(half) + half


def dot_nn(a, b):
    return jnp.dot(a, b, preferred_element_type=F32)


def clear(*arrays):
    for w in arrays:
        w[...] = jnp.zeros_like(w)


def inner_taps(v):
    half = v.shape[0] // 2
    even, odd = v[:half], v[half:]
    row = lax.broadcasted_iota(jnp.int32, even.shape, 0)
    after = jnp.where(row == half - 1, 0.0, pltpu.roll(even, half - 1, 0))
    before = jnp.where(row == 0, 0.0, pltpu.roll(odd, 1, 0))
    return jnp.concatenate([even, odd, after, before], axis=1).astype(BF16)


def fill(w, kernel, cin, first_in):
    C = kernel.shape[2]
    for q in range(2):
        for p in range(2):
            for a in range(4):
                for l, off in enumerate(OFFSETS):
                    kr, kcol = a - q, off - p + 1
                    if 0 <= kr < 3 and 0 <= kcol < 3:
                        at = (q * 2 + p) * C
                        lane = a * 4 * cin + l * cin
                        w[at : at + C, lane : lane + cin] = kernel[kr, kcol][:, first_in : first_in + cin]


def fine_weights(k1, k2, km, w1, wlast, wfirst, wnext, w2, wma, wmb):
    channels, C = k1.shape[2], k1.shape[3]
    wide = PER * channels
    clear(w1, wlast, wfirst, wnext, w2, wma, wmb)
    for p in range(2):
        for l, off in enumerate(OFFSETS):
            if not 0 <= off - p + 1 < 3:
                continue
            k = [k1[kr, off - p + 1] for kr in range(3)]
            lane = l * wide
            for r in range(PER):
                at = (r * 2 + p) * C
                for kr in range(3):
                    if 0 <= r + kr - 1 < PER:
                        to = lane + (r + kr - 1) * channels
                        w1[to : to + channels, at : at + C] = k[kr]
            end = lane + (PER - 1) * channels
            wlast[end : end + channels, p * C : (p + 1) * C] = k[0]
            wfirst[lane : lane + channels, p * C : (p + 1) * C] = k[0]
            wnext[lane : lane + channels, p * C : (p + 1) * C] = k[2]
    fill(w2, k2, C, 0)
    fill(wma, km, C, 0)
    fill(wmb, km, C, C)


def coarse_weights(kd, kc, ku, kp, wd, wc, wu, wp):
    C, C2 = kd.shape[2], kd.shape[3]
    COUT = kp.shape[0]
    clear(wd, wc, wu, wp)
    for a in range(3):
        for l, kcol in ((0, 1), (1, 2), (3, 0)):
            wd[a * 4 * C + l * C : a * 4 * C + (l + 1) * C] = kd[a, kcol]
        for s, kcol in enumerate((1, 2, 0)):
            wc[:, (a * 3 + s) * C2 : (a * 3 + s + 1) * C2] = kc[a, kcol]
    for q, rows in ((0, ((0, 1),)), (1, ((0, 0), (1, 2)))):
        for p, columns in ((0, ((0, 1),)), (1, ((0, 0), (1, 2)))):
            at = (q * 2 + p) * C
            for ri, kr in rows:
                for ci, kcol in columns:
                    lane = (ri * 2 + ci) * C2
                    wu[at : at + C, lane : lane + C2] = ku[kr, kcol]
    for g in range(4):
        wp[g * COUT : (g + 1) * COUT, g * C : (g + 1) * C] = kp[...].astype(F32)


def exchange_kernel(n, lat_ref, tab_hbm, k1_hbm, k2_hbm, kd_hbm, kc_hbm, ku_hbm, km_hbm, kp_hbm,
                    own_ref, halo_ref, pre_ref, w1, wlast, wfirst, wnext, w2, wd, wc, wu, wma, wmb, wp,
                    tab_ref, k1, k2, kd, kc, ku, km, kp, recv, edge, hot, edge_hot, edge_at, at_ref, fold_ref,
                    send_sem, recv_sem, own_sem, hsend, hrecv, load_sem):
    me = lax.axis_index("lon")
    group = lax.axis_index("groups")
    cols = recv.shape[3]
    height = tab_ref.shape[1]
    per = height // own_ref.shape[0]
    sub_rows = lat_ref.shape[1]
    channels = own_ref.shape[2] // per
    barrier = pltpu.get_barrier_semaphore()

    def greet(d, carry):
        pl.semaphore_signal(barrier, inc=1, device_id=(group, lax.rem(me + d, n)), device_id_type=MESH)
        return carry

    lax.fori_loop(1, n, greet, 0)
    mine = pltpu.make_async_copy(lat_ref.at[:, :, pl.ds(pl.multiple_of(me * cols, cols), cols)], recv.at[me], own_sem)
    mine.start()
    loads = [pltpu.make_async_copy(src, dst, load_sem.at[i]) for i, (src, dst) in enumerate((
        (tab_hbm, tab_ref), (k1_hbm, k1), (k2_hbm, k2), (kd_hbm, kd), (kc_hbm, kc), (ku_hbm, ku), (km_hbm, km), (kp_hbm, kp)))]
    for load in loads:
        load.start()
    pl.semaphore_wait(barrier, n - 1)

    def block_copy(target):
        return pltpu.make_async_remote_copy(
            src_ref=lat_ref.at[:, :, pl.ds(pl.multiple_of(target * cols, cols), cols)],
            dst_ref=recv.at[me],
            send_sem=send_sem,
            recv_sem=recv_sem,
            device_id=(group, target),
            device_id_type=MESH,
        )

    def send(k, carry):
        target = n - 4 - k // 4 * 4 + (me + k + 1) % 4

        @pl.when(target != me)
        def _():
            block_copy(target).start()

        return carry

    lax.fori_loop(0, n, send, 0)

    loads[0].wait()
    p = lax.broadcasted_iota(jnp.int32, (cols, cols), 0)
    w = lax.broadcasted_iota(jnp.int32, (cols, cols), 1)
    half = cols // 2
    perm = (w == jnp.where(p < half, 2 * p, 2 * p - cols + 1)).astype(F32).astype(BF16)
    rows_at = dot_nt(perm, tab_ref[0].astype(F32).astype(BF16)).astype(jnp.int32)
    cols_at = dot_nt(perm, (tab_ref[1] - me * cols).astype(F32).astype(BF16)).astype(jnp.int32)
    wide = per * channels
    lane = lax.broadcasted_iota(jnp.int32, (cols, wide), 1)
    wide_hot = lax.broadcasted_iota(jnp.int32, (cols, 2 * cols), 1)
    held = sub_rows * channels
    per_tile = wide // held
    spot = lane // held * sub_rows + lane % sub_rows
    pair = rows_at // (2 * sub_rows)
    col_key = cols_at + rows_at // sub_rows % 2 * cols
    row_key = pair * sub_rows + rows_at % sub_rows
    groups = own_ref.shape[0]
    strip = 2 * HALO
    ep = lax.broadcasted_iota(jnp.int32, (2 * strip, cols), 0)
    ew = lax.broadcasted_iota(jnp.int32, (2 * strip, cols), 1)
    first = jnp.where(ep < HALO, 2 * ep, 2 * (ep - HALO) + 1)
    last = jnp.where(ep < strip + HALO, 2 * (ep - strip) + 1, 2 * (ep - strip - HALO)) + cols - strip
    edge_perm = (ew == jnp.where(ep < strip, first, last)).astype(F32).astype(BF16)
    edge_rows = dot_nt(edge_perm, tab_ref[0].astype(F32).astype(BF16)).astype(jnp.int32)
    edge_cols = dot_nt(edge_perm, (tab_ref[1] - me * cols).astype(F32).astype(BF16)).astype(jnp.int32)
    edge_col_key = edge_cols + edge_rows // sub_rows % 2 * cols
    edge_row_key = edge_rows // (2 * sub_rows) * sub_rows + edge_rows % sub_rows
    edge_held = 2 * groups * strip

    def edge_of(keys, q, width):
        return jnp.concatenate([jnp.broadcast_to(keys[side * strip : (side + 1) * strip, g * per + q : g * per + q + 1], (strip, width))
                                for side in range(2) for g in range(groups)], axis=0)

    for q in range(per):
        edge_hot[q * edge_held : (q + 1) * edge_held] = (edge_of(edge_col_key, q, 2 * cols) == wide_hot[:edge_held]).astype(F32).astype(BF16)
        edge_at[q * edge_held : (q + 1) * edge_held] = edge_of(edge_row_key, q, wide) - spot[:edge_held]
    for h in range(height):
        hot[h * cols : (h + 1) * cols] = (col_key[:, h : h + 1] == wide_hot).astype(F32).astype(BF16)
        at_ref[h * cols : (h + 1) * cols] = jnp.broadcast_to(row_key[:, h : h + 1], (cols, wide)) - spot
    fi = lax.broadcasted_iota(jnp.int32, (per * wide, wide), 0)
    fo = lax.broadcasted_iota(jnp.int32, (per * wide, wide), 1)
    fold_ref[...] = ((fi // wide == fo // channels) & (fi % held // sub_rows == fo % channels)).astype(F32).astype(BF16)
    for load in loads[1:]:
        load.wait()
    coarse_weights(kd, kc, ku, kp, wd, wc, wu, wp)
    fine_weights(k1, k2, km, w1, wlast, wfirst, wnext, w2, wma, wmb)
    mine.wait()

    blocks = pltpu.make_async_remote_copy(
        src_ref=recv.at[pl.ds(0, n - 1)], dst_ref=recv.at[pl.ds(0, n - 1)], send_sem=send_sem, recv_sem=recv_sem,
        device_id=(group, lax.rem(me + 1, n)), device_id_type=MESH)
    blocks.wait_recv()

    def halo(src, dst, shift):
        return pltpu.make_async_remote_copy(
            src_ref=src, dst_ref=dst, send_sem=hsend, recv_sem=hrecv,
            device_id=(group, lax.rem(me + shift + 2 * n, n)), device_id_type=MESH)

    lead = groups * strip
    firsts, lasts = edge.at[pl.ds(0, lead)], edge.at[pl.ds(lead, lead)]

    def source_of():
        arrived = recv[...].reshape(n // 2, 2, held, cols)
        return jnp.concatenate([arrived[:, 0], arrived[:, 1]], axis=2).reshape(n // 2 * held, 2 * cols)

    tiles = n // 2 * held // wide

    def pick(got, at, q, count):
        one = jnp.zeros((count, wide), F32)
        for t in range(tiles):
            value = got[q * count : (q + 1) * count, t * wide : (t + 1) * wide]
            one = jnp.where(at == t * per_tile * sub_rows, value, one)
        return one.astype(BF16)

    got = dot_nt(edge_hot[...], source_of())
    picked = [pick(got, edge_at[q * edge_held : (q + 1) * edge_held], q, edge_held) for q in range(per)]
    edge[...] = jnp.dot(jnp.concatenate(picked, axis=1), fold_ref[...], preferred_element_type=F32).astype(BF16)
    for src, first_row, count, shift in (
        (lasts, cols + 4 * strip, lead, 1), (firsts, cols + 4 * strip + lead, lead, -1),
        (edge.at[pl.ds(lead, 2 * strip)], cols, 2 * strip, n // 2 + 1), (edge.at[pl.ds(0, 2 * strip)], cols + 2 * strip, 2 * strip, n // 2 - 1),
    ):
        halo(src, halo_ref.at[pl.ds(first_row, count)], shift).start()

    @pl.when(me >= 0)
    def _():
        source = source_of()
        for g in range(groups):
            got = dot_nt(hot[g * per * cols : (g + 1) * per * cols], source)
            picked = [pick(got, at_ref[(g * per + q) * cols : (g * per + q + 1) * cols], q, cols) for q in range(per)]
            own_ref[g] = jnp.dot(jnp.concatenate(picked, axis=1), fold_ref[...], preferred_element_type=F32).astype(BF16)
            if g == 0:
                halo(own_ref.at[0], halo_ref.at[pl.ds(0, cols)], n // 2).start()

    middle = jnp.concatenate([inner_taps(own_ref[g].astype(F32)) for g in range(groups)], axis=0)
    half, pair = cols // 2, 2 * k1.shape[3]
    base = dot_nn(middle, w1[...])
    above = dot_nn(middle[: (groups - 1) * half], wlast[...])
    below = dot_nn(middle[half:], wnext[...])
    for g in range(groups):
        for r in range(per):
            v = base[g * half : (g + 1) * half, r * pair : (r + 1) * pair]
            if r == 0 and g > 0:
                v = v + above[(g - 1) * half : g * half]
            if r == per - 1 and g < groups - 1:
                v = v + below[g * half : (g + 1) * half]
            if g + r > 0:
                v = jnp.concatenate([v[:strip], silu(v[strip : half - strip]), v[half - strip :]], axis=0)
            pre_ref[g * per + r] = v
    blocks.wait_send()
    every = halo(halo_ref, halo_ref, 1)
    every.wait_send()
    every.wait_recv()


def unet_kernel(own_ref, halo_ref, pre_ref, w1, wlast, wfirst, wnext, w2, wd, wc, wu, wma, wmb, wp, out_ref, x1, x2, x3, xc, xu):
    groups, cols, wide = own_ref.shape
    height = groups * PER
    channels = wide // PER
    half = cols // 2
    J = half + 2 * HALO
    C = w2.shape[0] // 4
    C2 = wd.shape[1]
    COUT = wp.shape[0] // 4
    pairs = height // 2
    AB = pairs + 1

    strip = 2 * HALO
    upper = lax.broadcasted_iota(jnp.int32, (strip, wide), 0) < HALO

    def spread(g, l, r):
        even = jnp.concatenate([g[:half], jnp.where(upper, r, l)], axis=0)
        odd = jnp.concatenate([g[half:], pltpu.roll(jnp.where(upper, l, r), HALO, 0)], axis=0)
        return jnp.concatenate([even, odd, pltpu.roll(even, J - 1, 0), pltpu.roll(odd, 1, 0)], axis=1).astype(BF16)

    around = halo_ref[...].astype(F32)
    corners, sides = around[cols : cols + 4 * strip], around[cols + 4 * strip :]
    row = lax.broadcasted_iota(jnp.int32, (strip, wide), 0)
    none = jnp.zeros((strip, wide), F32)

    def rim(g, l, r):
        even, odd = jnp.where(upper, r, l), pltpu.roll(jnp.where(upper, l, r), HALO, 0)
        after = jnp.where(row == strip - 1, g[0:1], pltpu.roll(even, strip - 1, 0))
        before = jnp.where(row == 0, g[cols - 1 : cols], pltpu.roll(odd, 1, 0))
        ring = jnp.concatenate([even, odd, after, before], axis=1)
        ends = jnp.concatenate([none, none, jnp.where(row == 0, even, 0.0), jnp.where(row == strip - 1, odd, 0.0)], axis=1)
        return jnp.concatenate([ring, ends], axis=0).astype(BF16)

    own = [own_ref[g].astype(F32) for g in range(groups)]
    lefts = [sides[g * strip : (g + 1) * strip] for g in range(groups)]
    rights = [sides[(groups + g) * strip : (groups + g + 1) * strip] for g in range(groups)]
    rims = jnp.concatenate([rim(own[g], lefts[g], rights[g]) for g in range(groups)], axis=0)
    top = spread(own[0], lefts[0], rights[0])
    across = spread(around[:cols], corners[:strip], corners[2 * strip : 3 * strip])

    def neighbours(v):
        count = v.shape[0]
        v = v.reshape(count // J, J, v.shape[1])
        lane = lax.broadcasted_iota(jnp.int32, v.shape, 2)
        other = jnp.where(lane < C, pltpu.roll(v, J - 1, 1), pltpu.roll(v, 1, 1))
        return jnp.concatenate([v, other], axis=2).astype(BF16)

    def store_pair(x, i0, count, s):
        x[pl.ds(i0, count), 1] = neighbours(s[:, : 2 * C])
        x[pl.ds(i0 + 1, count), 0] = neighbours(s[:, 2 * C :])

    def wrap(x):
        x[0, 0] = x[AB, 1]
        x[AB, 0] = x[0, 1]
        x[AB - 1, 1] = jnp.zeros(x.shape[2:], BF16)

    def taps(x, i0, count, a, width):
        v = x[pl.ds(i0 + a // 2, count), a % 2, 0:width]
        return v.reshape(count * width, v.shape[-1])

    B = 8
    BM = 4

    def own_loop(steps, body):
        for t in range(steps):
            body(t)

    R = 2 * strip
    base = dot_nn(rims, w1[...])
    above = dot_nn(rims[: (groups - 1) * R], wlast[...])
    below = dot_nn(rims[R:], wnext[...])
    own_top = dot_nn(across, wfirst[...])
    anti_top = dot_nn(top, wfirst[...])
    anti = dot_nn(across, w1[...])
    for g in range(groups):
        for r in range(PER):
            e = base[g * R : (g + 1) * R, r * 2 * C : (r + 1) * 2 * C]
            if r == 0 and g > 0:
                e = e + above[(g - 1) * R : g * R]
            if r == PER - 1 and g < groups - 1:
                e = e + below[g * R : (g + 1) * R]
            ring, ends = e[:strip], e[strip:]
            v = pre_ref[g * PER + r]
            head = v[:strip] + jnp.where(row == 0, pltpu.roll(ends, 1, 0), 0.0)
            tail = v[half - strip :] + jnp.where(row == strip - 1, pltpu.roll(ends, strip - 1, 0), 0.0)
            inner = v[strip : half - strip]
            if g + r > 0:
                v = silu(jnp.concatenate([head, tail, ring], axis=0))
                v = jnp.concatenate([v[:strip], inner, v[strip:]], axis=0)
            else:
                v = silu(jnp.concatenate([head, inner, tail, ring], axis=0) + own_top)
            slot = g * PER + r + 1
            x1[slot // 2, slot % 2] = neighbours(v)[0]
    for r in range(PER):
        slot = groups * PER + r + 3
        if slot // 2 < x1.shape[0]:
            v = anti[:, r * 2 * C : (r + 1) * 2 * C]
            x1[slot // 2, slot % 2] = neighbours(silu(v + anti_top if r == 0 else v))[0]
    wrap(x1)

    def second(i0, count):
        acc = dot_nt(jnp.concatenate([taps(x1, i0, count, a, J) for a in range(4)], axis=1), w2[...])
        store_pair(x2, i0, count, silu(acc))

    second(AB, 2)
    own_loop(pairs // B, lambda t: second(t * B, B))
    wrap(x2)

    def shifts(v, both):
        v = v.reshape(v.shape[0] // J, J, v.shape[1])
        parts = [v, pltpu.roll(v, J - 1, 1)]
        if both:
            parts.append(pltpu.roll(v, 1, 1))
        return jnp.concatenate(parts, axis=2).astype(BF16)

    def down(i0, slot, count):
        acc = dot_nn(jnp.concatenate([taps(x2, i0, count, a, J) for a in range(3)], axis=1), wd[...])
        xc[pl.ds(slot, count)] = shifts(silu(acc), True)

    down(AB, pairs + 3, 2)
    own_loop(pairs // B, lambda t: down(t * B, t * B + 1, B))
    xc[0] = xc[pairs + 3]
    xc[pairs + 2] = xc[1]
    xc[pairs + 1] = jnp.zeros(xc.shape[1:], BF16)

    def coarse(i0, slot, count):
        acc = dot_nt(jnp.concatenate([xc[pl.ds(i0 + a, count)].reshape(count * J, 3 * C2) for a in range(3)], axis=1), wc[...])
        xu[pl.ds(slot, count)] = shifts(silu(acc), False)

    coarse(pairs + 2, pairs + 1, 1)
    own_loop(pairs // B, lambda t: coarse(t * B, t * B, B))
    xu[pairs] = jnp.zeros(xu.shape[1:], BF16)

    def up(i0, count):
        return silu(dot_nt(jnp.concatenate([xu[pl.ds(i0 + a, count)].reshape(count * J, 2 * C2) for a in range(2)], axis=1), wu[...]))

    def up_own(t):
        store_pair(x3, t * B, B, up(t * B, B))

    own_loop(pairs // B, up_own)
    v = xu[pairs + 1]
    x3[0, 0] = neighbours(silu(dot_nt(v, wu[0 : 2 * C, : 2 * C2])))[0]
    x3[AB - 1, 1] = jnp.zeros(x3.shape[2:], BF16)

    p = lax.broadcasted_iota(jnp.int32, (cols, cols), 0)
    w = lax.broadcasted_iota(jnp.int32, (cols, cols), 1)
    unperm = (w == jnp.where(p < half, 2 * p, 2 * p - cols + 1)).astype(F32).astype(BF16)
    unperm = jnp.concatenate([unperm, unperm], axis=0)
    wpb = wp[...].astype(BF16)
    plain = [own_ref[g].astype(F32).T for g in range(groups)]

    def merge(i0, count):
        tiles = [taps(x, i0, count, a, half) for x in (x2, x3) for a in range(4)]
        return silu(dot_nt(jnp.concatenate(tiles, axis=1), jnp.concatenate([wma[...], wmb[...]], axis=1))).astype(BF16)

    merged = [merge(t * BM, BM) for t in range(pairs // BM)]
    lines = []
    for t in range(pairs // BM):
        update = dot_nt(wpb, merged[t])
        for b in range(BM):
            u = update[:, b * half : (b + 1) * half]
            for q in range(2):
                line = jnp.concatenate([u[2 * q * COUT : (2 * q + 1) * COUT], u[(2 * q + 1) * COUT : (2 * q + 2) * COUT]], axis=1)
                h = 2 * (t * BM + b) + q
                at = (h % PER) * channels
                lines.append(line + plain[h // PER][at : at + COUT])
    lines = jnp.concatenate(lines, axis=0)
    high = lines.astype(BF16)
    low = (lines - high.astype(F32)).astype(BF16)
    woven = dot_nn(jnp.concatenate([high, low], axis=1), unperm)
    for h in range(height):
        out_ref[:, h, :] = woven[h * COUT : (h + 1) * COUT]


def shards(latlon, table, k1, k2, kd, kc, ku, km, kp):
    n = lax.axis_size("lon")
    k1, kd = jnp.swapaxes(k1, 2, 3), jnp.swapaxes(kd, 2, 3)
    channels, sub_rows, width = latlon.shape
    height, cols = table.shape[1], table.shape[2]
    vm = pl.BlockSpec(memory_space=pltpu.VMEM)
    groups = height // PER
    sides = 2 * groups * 2 * HALO
    around = jax.ShapeDtypeStruct((cols + 8 * HALO + sides, PER * channels), BF16)
    C, C2, COUT = k1.shape[3], kd.shape[3], kp.shape[0]
    weights = (
        jax.ShapeDtypeStruct((4 * PER * channels, 2 * C * PER), BF16),
        jax.ShapeDtypeStruct((4 * PER * channels, 2 * C), BF16),
        jax.ShapeDtypeStruct((4 * PER * channels, 2 * C), BF16),
        jax.ShapeDtypeStruct((4 * PER * channels, 2 * C), BF16),
        jax.ShapeDtypeStruct((4 * C, 16 * C), BF16),
        jax.ShapeDtypeStruct((12 * C, C2), BF16),
        jax.ShapeDtypeStruct((C2, 9 * C2), BF16),
        jax.ShapeDtypeStruct((4 * C, 4 * C2), BF16),
        jax.ShapeDtypeStruct((4 * C, 16 * C), BF16),
        jax.ShapeDtypeStruct((4 * C, 16 * C), BF16),
        jax.ShapeDtypeStruct((4 * COUT, 4 * C), F32),
    )
    ready = pl.pallas_call(
        functools.partial(exchange_kernel, n),
        out_shape=(jax.ShapeDtypeStruct((groups, cols, PER * channels), BF16), around,
                   jax.ShapeDtypeStruct((height, cols // 2, 2 * C), F32)) + weights,
        in_specs=[pl.BlockSpec(memory_space=pltpu.HBM)] * 9,
        out_specs=(vm,) * 14,
        scratch_shapes=[
            pltpu.VMEM(table.shape, table.dtype),
        ] + [pltpu.VMEM(k.shape, BF16) for k in (k1, k2, kd, kc, ku, km, kp)] + [
            pltpu.VMEM((n, channels, sub_rows, cols), BF16),
            pltpu.VMEM((sides, PER * channels), BF16),
            pltpu.VMEM((height * cols, 2 * cols), BF16),
            pltpu.VMEM((PER * sides, 2 * cols), BF16),
            pltpu.VMEM((PER * sides, PER * channels), jnp.int32),
            pltpu.VMEM((height * cols, PER * channels), jnp.int32),
            pltpu.VMEM((PER * PER * channels, PER * channels), BF16),
            pltpu.SemaphoreType.DMA,
            pltpu.SemaphoreType.DMA,
            pltpu.SemaphoreType.DMA,
            pltpu.SemaphoreType.DMA,
            pltpu.SemaphoreType.DMA,
            pltpu.SemaphoreType.DMA((8,)),
        ],
        compiler_params=pltpu.CompilerParams(collective_id=0, has_side_effects=True, vmem_limit_bytes=32 * 2**20),
        name="exchange",
    )(*(pltpu.with_memory_space_constraint(v, pltpu.HBM) for v in (latlon, table, k1, k2, kd, kc, ku, km, kp)))
    J = cols // 2 + 2 * HALO
    pairs = height // 2
    return pl.pallas_call(
        unet_kernel,
        out_shape=jax.ShapeDtypeStruct((COUT, height, cols), F32),
        in_specs=[vm] * 14,
        out_specs=vm,
        scratch_shapes=[
            pltpu.VMEM((pairs + 5, 2, J, 4 * C), BF16),
            pltpu.VMEM((pairs + 4, 2, J, 4 * C), BF16),
            pltpu.VMEM((pairs + 1, 2, J, 4 * C), BF16),
            pltpu.VMEM((pairs + 5, J, 3 * C2), BF16),
            pltpu.VMEM((pairs + 2, J, 2 * C2), BF16),
        ],
        compiler_params=pltpu.CompilerParams(vmem_limit_bytes=32 * 2**20),
        name="unet",
    )(*ready)


def solution(mesh):
    return jax.shard_map(
        shards,
        mesh=mesh,
        in_specs=(P("groups", "lon", None), P(None, None, "lon")) + (P(),) * 7,
        out_specs=P("groups", None, "lon"),
        check_vma=False,
    )
```

```python
import functools

import jax
import jax.numpy as jnp
from jax import lax
from jax.experimental import pallas as pl
from jax.experimental.pallas import tpu as pltpu
from jax.sharding import PartitionSpec as P

MESH = pl.DeviceIdType.MESH
F32 = jnp.float32
BF16 = jnp.bfloat16
HALO = 4
PER = 8
OFFSETS = (0, 1, 2, -1)
NT = (((1,), (1,)), ((), ()))


def dot_nt(a, b):
    return lax.dot_general(a, b, NT, preferred_element_type=F32)


def silu(x):
    half = 0.5 * x
    return half * jnp.tanh(half) + half


def dot_nn(a, b):
    return jnp.dot(a, b, preferred_element_type=F32)


def clear(*arrays):
    for w in arrays:
        w[...] = jnp.zeros_like(w)


def inner_taps(v):
    half = v.shape[0] // 2
    even, odd = v[:half], v[half:]
    row = lax.broadcasted_iota(jnp.int32, even.shape, 0)
    after = jnp.where(row == half - 1, 0.0, pltpu.roll(even, half - 1, 0))
    before = jnp.where(row == 0, 0.0, pltpu.roll(odd, 1, 0))
    return jnp.concatenate([even, odd, after, before], axis=1).astype(BF16)


def fill(w, kernel, cin, first_in):
    C = kernel.shape[2]
    for q in range(2):
        for p in range(2):
            for a in range(4):
                for l, off in enumerate(OFFSETS):
                    kr, kcol = a - q, off - p + 1
                    if 0 <= kr < 3 and 0 <= kcol < 3:
                        at = (q * 2 + p) * C
                        lane = a * 4 * cin + l * cin
                        w[at : at + C, lane : lane + cin] = kernel[kr, kcol][:, first_in : first_in + cin]


def fine_weights(k1, k2, km, w1, wlast, wfirst, wnext, w2, wma, wmb):
    channels, C = k1.shape[2], k1.shape[3]
    wide = PER * channels
    clear(w1, wlast, wfirst, wnext, w2, wma, wmb)
    for p in range(2):
        for l, off in enumerate(OFFSETS):
            if not 0 <= off - p + 1 < 3:
                continue
            k = [k1[kr, off - p + 1] for kr in range(3)]
            lane = l * wide
            for r in range(PER):
                at = (r * 2 + p) * C
                for kr in range(3):
                    if 0 <= r + kr - 1 < PER:
                        to = lane + (r + kr - 1) * channels
                        w1[to : to + channels, at : at + C] = k[kr]
            end = lane + (PER - 1) * channels
            wlast[end : end + channels, p * C : (p + 1) * C] = k[0]
            wfirst[lane : lane + channels, p * C : (p + 1) * C] = k[0]
            wnext[lane : lane + channels, p * C : (p + 1) * C] = k[2]
    fill(w2, k2, C, 0)
    fill(wma, km, C, 0)
    fill(wmb, km, C, C)


def coarse_weights(kd, kc, ku, kp, wd, wc, wu, wp):
    C, C2 = kd.shape[2], kd.shape[3]
    COUT = kp.shape[0]
    clear(wd, wc, wu, wp)
    for a in range(3):
        for l, kcol in ((0, 1), (1, 2), (3, 0)):
            wd[a * 4 * C + l * C : a * 4 * C + (l + 1) * C] = kd[a, kcol]
        for s, kcol in enumerate((1, 2, 0)):
            wc[:, (a * 3 + s) * C2 : (a * 3 + s + 1) * C2] = kc[a, kcol]
    for q, rows in ((0, ((0, 1),)), (1, ((0, 0), (1, 2)))):
        for p, columns in ((0, ((0, 1),)), (1, ((0, 0), (1, 2)))):
            at = (q * 2 + p) * C
            for ri, kr in rows:
                for ci, kcol in columns:
                    lane = (ri * 2 + ci) * C2
                    wu[at : at + C, lane : lane + C2] = ku[kr, kcol]
    for g in range(4):
        wp[g * COUT : (g + 1) * COUT, g * C : (g + 1) * C] = kp[...].astype(F32)


def exchange_kernel(n, lat_ref, tab_hbm, k1_hbm, k2_hbm, kd_hbm, kc_hbm, ku_hbm, km_hbm, kp_hbm,
                    own_ref, halo_ref, pre_ref, rest_ref, w1, wlast, wfirst, wnext, w2, wd, wc, wu, wma, wmb, wp,
                    tab_ref, k1, k2, kd, kc, ku, km, kp, recv, edge, hot, edge_hot, edge_at, at_ref, fold_ref,
                    send_sem, recv_sem, own_sem, hsend, hrecv, load_sem):
    me = lax.axis_index("lon")
    group = lax.axis_index("groups")
    cols = recv.shape[3]
    height = tab_ref.shape[1]
    per = height // own_ref.shape[0]
    sub_rows = lat_ref.shape[1]
    channels = own_ref.shape[2] // per
    barrier = pltpu.get_barrier_semaphore()

    def greet(d, carry):
        pl.semaphore_signal(barrier, inc=1, device_id=(group, lax.rem(me + d, n)), device_id_type=MESH)
        return carry

    lax.fori_loop(1, n, greet, 0)
    mine = pltpu.make_async_copy(lat_ref.at[:, :, pl.ds(pl.multiple_of(me * cols, cols), cols)], recv.at[me], own_sem)
    mine.start()
    loads = [pltpu.make_async_copy(src, dst, load_sem.at[i]) for i, (src, dst) in enumerate((
        (tab_hbm, tab_ref), (k1_hbm, k1), (k2_hbm, k2), (kd_hbm, kd), (kc_hbm, kc), (ku_hbm, ku), (km_hbm, km), (kp_hbm, kp)))]
    for load in loads:
        load.start()
    pl.semaphore_wait(barrier, n - 1)

    def block_copy(target):
        return pltpu.make_async_remote_copy(
            src_ref=lat_ref.at[:, :, pl.ds(pl.multiple_of(target * cols, cols), cols)],
            dst_ref=recv.at[me],
            send_sem=send_sem,
            recv_sem=recv_sem,
            device_id=(group, target),
            device_id_type=MESH,
        )

    def send(k, carry):
        target = n - 4 - k // 4 * 4 + (me + k + 1) % 4

        @pl.when(target != me)
        def _():
            block_copy(target).start()

        return carry

    lax.fori_loop(0, n, send, 0)

    loads[0].wait()
    p = lax.broadcasted_iota(jnp.int32, (cols, cols), 0)
    w = lax.broadcasted_iota(jnp.int32, (cols, cols), 1)
    half = cols // 2
    perm = (w == jnp.where(p < half, 2 * p, 2 * p - cols + 1)).astype(F32).astype(BF16)
    rows_at = dot_nt(perm, tab_ref[0].astype(F32).astype(BF16)).astype(jnp.int32)
    cols_at = dot_nt(perm, (tab_ref[1] - me * cols).astype(F32).astype(BF16)).astype(jnp.int32)
    wide = per * channels
    lane = lax.broadcasted_iota(jnp.int32, (cols, wide), 1)
    wide_hot = lax.broadcasted_iota(jnp.int32, (cols, 2 * cols), 1)
    held = sub_rows * channels
    per_tile = wide // held
    spot = lane // held * sub_rows + lane % sub_rows
    pair = rows_at // (2 * sub_rows)
    col_key = cols_at + rows_at // sub_rows % 2 * cols
    row_key = pair * sub_rows + rows_at % sub_rows
    groups = own_ref.shape[0]
    strip = 2 * HALO
    ep = lax.broadcasted_iota(jnp.int32, (2 * strip, cols), 0)
    ew = lax.broadcasted_iota(jnp.int32, (2 * strip, cols), 1)
    first = jnp.where(ep < HALO, 2 * ep, 2 * (ep - HALO) + 1)
    last = jnp.where(ep < strip + HALO, 2 * (ep - strip) + 1, 2 * (ep - strip - HALO)) + cols - strip
    edge_perm = (ew == jnp.where(ep < strip, first, last)).astype(F32).astype(BF16)
    edge_rows = dot_nt(edge_perm, tab_ref[0].astype(F32).astype(BF16)).astype(jnp.int32)
    edge_cols = dot_nt(edge_perm, (tab_ref[1] - me * cols).astype(F32).astype(BF16)).astype(jnp.int32)
    edge_col_key = edge_cols + edge_rows // sub_rows % 2 * cols
    edge_row_key = edge_rows // (2 * sub_rows) * sub_rows + edge_rows % sub_rows
    edge_held = 2 * groups * strip

    def edge_of(keys, q, width):
        return jnp.concatenate([jnp.broadcast_to(keys[side * strip : (side + 1) * strip, g * per + q : g * per + q + 1], (strip, width))
                                for side in range(2) for g in range(groups)], axis=0)

    for q in range(per):
        edge_hot[q * edge_held : (q + 1) * edge_held] = (edge_of(edge_col_key, q, 2 * cols) == wide_hot[:edge_held]).astype(F32).astype(BF16)
        edge_at[q * edge_held : (q + 1) * edge_held] = edge_of(edge_row_key, q, wide) - spot[:edge_held]
    for h in range(height):
        hot[h * cols : (h + 1) * cols] = (col_key[:, h : h + 1] == wide_hot).astype(F32).astype(BF16)
        at_ref[h * cols : (h + 1) * cols] = jnp.broadcast_to(row_key[:, h : h + 1], (cols, wide)) - spot
    fi = lax.broadcasted_iota(jnp.int32, (per * wide, wide), 0)
    fo = lax.broadcasted_iota(jnp.int32, (per * wide, wide), 1)
    fold_ref[...] = ((fi // wide == fo // channels) & (fi % held // sub_rows == fo % channels)).astype(F32).astype(BF16)
    for load in loads[1:]:
        load.wait()
    coarse_weights(kd, kc, ku, kp, wd, wc, wu, wp)
    fine_weights(k1, k2, km, w1, wlast, wfirst, wnext, w2, wma, wmb)
    mine.wait()

    blocks = pltpu.make_async_remote_copy(
        src_ref=recv.at[pl.ds(0, n - 1)], dst_ref=recv.at[pl.ds(0, n - 1)], send_sem=send_sem, recv_sem=recv_sem,
        device_id=(group, lax.rem(me + 1, n)), device_id_type=MESH)
    blocks.wait_recv()

    def halo(src, dst, shift):
        return pltpu.make_async_remote_copy(
            src_ref=src, dst_ref=dst, send_sem=hsend, recv_sem=hrecv,
            device_id=(group, lax.rem(me + shift + 2 * n, n)), device_id_type=MESH)

    lead = groups * strip
    firsts, lasts = edge.at[pl.ds(0, lead)], edge.at[pl.ds(lead, lead)]

    def source_of():
        arrived = recv[...].reshape(n // 2, 2, held, cols)
        return jnp.concatenate([arrived[:, 0], arrived[:, 1]], axis=2).reshape(n // 2 * held, 2 * cols)

    tiles = n // 2 * held // wide

    def pick(got, at, q, count):
        one = jnp.zeros((count, wide), F32)
        for t in range(tiles):
            value = got[q * count : (q + 1) * count, t * wide : (t + 1) * wide]
            one = jnp.where(at == t * per_tile * sub_rows, value, one)
        return one.astype(BF16)

    got = dot_nt(edge_hot[...], source_of())
    picked = [pick(got, edge_at[q * edge_held : (q + 1) * edge_held], q, edge_held) for q in range(per)]
    edge[...] = jnp.dot(jnp.concatenate(picked, axis=1), fold_ref[...], preferred_element_type=F32).astype(BF16)
    for src, first_row, count, shift in (
        (lasts, cols + 4 * strip, lead, 1), (firsts, cols + 4 * strip + lead, lead, -1),
        (edge.at[pl.ds(lead, 2 * strip)], cols, 2 * strip, n // 2 + 1), (edge.at[pl.ds(0, 2 * strip)], cols + 2 * strip, 2 * strip, n // 2 - 1),
    ):
        halo(src, halo_ref.at[pl.ds(first_row, count)], shift).start()

    @pl.when(me >= 0)
    def _():
        source = source_of()
        for g in range(groups):
            got = dot_nt(hot[g * per * cols : (g + 1) * per * cols], source)
            picked = [pick(got, at_ref[(g * per + q) * cols : (g * per + q + 1) * cols], q, cols) for q in range(per)]
            own_ref[g] = jnp.dot(jnp.concatenate(picked, axis=1), fold_ref[...], preferred_element_type=F32).astype(BF16)
            if g == 0:
                halo(own_ref.at[0], halo_ref.at[pl.ds(0, cols)], n // 2).start()

    middle = jnp.concatenate([inner_taps(own_ref[g].astype(F32)) for g in range(groups)], axis=0)
    half, pair = cols // 2, 2 * k1.shape[3]
    base = dot_nn(middle, w1[...])
    above = dot_nn(middle[: (groups - 1) * half], wlast[...])
    below = dot_nn(middle[half:], wnext[...])
    for g in range(groups):
        for r in range(per):
            v = base[g * half : (g + 1) * half, r * pair : (r + 1) * pair]
            if r == 0 and g > 0:
                v = v + above[(g - 1) * half : g * half]
            if r == per - 1 and g < groups - 1:
                v = v + below[g * half : (g + 1) * half]
            if g + r > 0:
                v = jnp.concatenate([v[:strip], silu(v[strip : half - strip]), v[half - strip :]], axis=0)
            pre_ref[g * per + r] = v
    outputs = wp.shape[0] // 4
    flat = [own_ref[g].astype(F32).T for g in range(groups)]
    kept = [flat[h // per][h % per * channels : h % per * channels + outputs] for h in range(height)]
    at = lax.broadcasted_iota(jnp.int32, (cols, cols), 0)
    unperm = (wide_hot[:, :cols] == jnp.where(at < half, 2 * at, 2 * at - cols + 1)).astype(F32).astype(BF16)
    rest_ref[...] = dot_nn(jnp.concatenate(kept, axis=0).astype(BF16), unperm)
    blocks.wait_send()
    every = halo(halo_ref, halo_ref, 1)
    every.wait_send()
    every.wait_recv()


def unet_kernel(own_ref, halo_ref, pre_ref, rest_ref, w1, wlast, wfirst, wnext, w2, wd, wc, wu, wma, wmb, wp, out_ref, x1, x2, x3, xc, xu):
    groups, cols, wide = own_ref.shape
    height = groups * PER
    channels = wide // PER
    half = cols // 2
    J = half + 2 * HALO
    C = w2.shape[0] // 4
    C2 = wd.shape[1]
    COUT = wp.shape[0] // 4
    pairs = height // 2
    AB = pairs + 1

    strip = 2 * HALO
    upper = lax.broadcasted_iota(jnp.int32, (strip, wide), 0) < HALO

    def spread(g, l, r):
        even = jnp.concatenate([g[:half], jnp.where(upper, r, l)], axis=0)
        odd = jnp.concatenate([g[half:], pltpu.roll(jnp.where(upper, l, r), HALO, 0)], axis=0)
        return jnp.concatenate([even, odd, pltpu.roll(even, J - 1, 0), pltpu.roll(odd, 1, 0)], axis=1).astype(BF16)

    around = halo_ref[...].astype(F32)
    corners, sides = around[cols : cols + 4 * strip], around[cols + 4 * strip :]
    row = lax.broadcasted_iota(jnp.int32, (strip, wide), 0)
    none = jnp.zeros((strip, wide), F32)

    def rim(g, l, r):
        even, odd = jnp.where(upper, r, l), pltpu.roll(jnp.where(upper, l, r), HALO, 0)
        after = jnp.where(row == strip - 1, g[0:1], pltpu.roll(even, strip - 1, 0))
        before = jnp.where(row == 0, g[cols - 1 : cols], pltpu.roll(odd, 1, 0))
        ring = jnp.concatenate([even, odd, after, before], axis=1)
        ends = jnp.concatenate([none, none, jnp.where(row == 0, even, 0.0), jnp.where(row == strip - 1, odd, 0.0)], axis=1)
        return jnp.concatenate([ring, ends], axis=0).astype(BF16)

    own = [own_ref[g].astype(F32) for g in range(groups)]
    lefts = [sides[g * strip : (g + 1) * strip] for g in range(groups)]
    rights = [sides[(groups + g) * strip : (groups + g + 1) * strip] for g in range(groups)]
    rims = jnp.concatenate([rim(own[g], lefts[g], rights[g]) for g in range(groups)], axis=0)
    top = spread(own[0], lefts[0], rights[0])
    across = spread(around[:cols], corners[:strip], corners[2 * strip : 3 * strip])

    def neighbours(v):
        count = v.shape[0]
        v = v.reshape(count // J, J, v.shape[1])
        lane = lax.broadcasted_iota(jnp.int32, v.shape, 2)
        other = jnp.where(lane < C, pltpu.roll(v, J - 1, 1), pltpu.roll(v, 1, 1))
        return jnp.concatenate([v, other], axis=2).astype(BF16)

    def store_pair(x, i0, count, s):
        x[pl.ds(i0, count), 1] = neighbours(s[:, : 2 * C])
        x[pl.ds(i0 + 1, count), 0] = neighbours(s[:, 2 * C :])

    def wrap(x):
        x[0, 0] = x[AB, 1]
        x[AB, 0] = x[0, 1]
        x[AB - 1, 1] = jnp.zeros(x.shape[2:], BF16)

    def taps(x, i0, count, a, width):
        v = x[pl.ds(i0 + a // 2, count), a % 2, 0:width]
        return v.reshape(count * width, v.shape[-1])

    B = 8
    BM = 4

    def own_loop(steps, body):
        for t in range(steps):
            body(t)

    R = 2 * strip
    base = dot_nn(rims, w1[...])
    above = dot_nn(rims[: (groups - 1) * R], wlast[...])
    below = dot_nn(rims[R:], wnext[...])
    own_top = dot_nn(across, wfirst[...])
    anti_top = dot_nn(top, wfirst[...])
    anti = dot_nn(across, w1[...])
    for g in range(groups):
        for r in range(PER):
            e = base[g * R : (g + 1) * R, r * 2 * C : (r + 1) * 2 * C]
            if r == 0 and g > 0:
                e = e + above[(g - 1) * R : g * R]
            if r == PER - 1 and g < groups - 1:
                e = e + below[g * R : (g + 1) * R]
            ring, ends = e[:strip], e[strip:]
            v = pre_ref[g * PER + r]
            head = v[:strip] + jnp.where(row == 0, pltpu.roll(ends, 1, 0), 0.0)
            tail = v[half - strip :] + jnp.where(row == strip - 1, pltpu.roll(ends, strip - 1, 0), 0.0)
            inner = v[strip : half - strip]
            if g + r > 0:
                v = silu(jnp.concatenate([head, tail, ring], axis=0))
                v = jnp.concatenate([v[:strip], inner, v[strip:]], axis=0)
            else:
                v = silu(jnp.concatenate([head, inner, tail, ring], axis=0) + own_top)
            slot = g * PER + r + 1
            x1[slot // 2, slot % 2] = neighbours(v)[0]
    for r in range(PER):
        slot = groups * PER + r + 3
        if slot // 2 < x1.shape[0]:
            v = anti[:, r * 2 * C : (r + 1) * 2 * C]
            x1[slot // 2, slot % 2] = neighbours(silu(v + anti_top if r == 0 else v))[0]
    wrap(x1)

    def second(i0, count):
        acc = dot_nt(jnp.concatenate([taps(x1, i0, count, a, J) for a in range(4)], axis=1), w2[...])
        store_pair(x2, i0, count, silu(acc))

    second(AB, 2)
    own_loop(pairs // B, lambda t: second(t * B, B))
    wrap(x2)

    def shifts(v, both):
        v = v.reshape(v.shape[0] // J, J, v.shape[1])
        parts = [v, pltpu.roll(v, J - 1, 1)]
        if both:
            parts.append(pltpu.roll(v, 1, 1))
        return jnp.concatenate(parts, axis=2).astype(BF16)

    def down(i0, slot, count):
        acc = dot_nn(jnp.concatenate([taps(x2, i0, count, a, J) for a in range(3)], axis=1), wd[...])
        xc[pl.ds(slot, count)] = shifts(silu(acc), True)

    own_loop(pairs // B, lambda t: down(t * B, t * B + 1, B))
    down(AB, pairs + 3, 2)
    xc[0] = xc[pairs + 3]
    xc[pairs + 2] = xc[1]
    xc[pairs + 1] = jnp.zeros(xc.shape[1:], BF16)

    def coarse(i0, slot, count):
        acc = dot_nt(jnp.concatenate([xc[pl.ds(i0 + a, count)].reshape(count * J, 3 * C2) for a in range(3)], axis=1), wc[...])
        xu[pl.ds(slot, count)] = shifts(silu(acc), False)

    own_loop(pairs // B, lambda t: coarse(t * B, t * B, B))
    coarse(pairs + 2, pairs + 1, 1)
    xu[pairs] = jnp.zeros(xu.shape[1:], BF16)

    def up(i0, count):
        return silu(dot_nt(jnp.concatenate([xu[pl.ds(i0 + a, count)].reshape(count * J, 2 * C2) for a in range(2)], axis=1), wu[...]))

    def up_own(t):
        store_pair(x3, t * B, B, up(t * B, B))

    own_loop(pairs // B, up_own)
    v = xu[pairs + 1]
    x3[0, 0] = neighbours(silu(dot_nt(v, wu[0 : 2 * C, : 2 * C2])))[0]
    x3[AB - 1, 1] = jnp.zeros(x3.shape[2:], BF16)

    p = lax.broadcasted_iota(jnp.int32, (cols, cols), 0)
    w = lax.broadcasted_iota(jnp.int32, (cols, cols), 1)
    unperm = (w == jnp.where(p < half, 2 * p, 2 * p - cols + 1)).astype(F32).astype(BF16)
    unperm = jnp.concatenate([unperm, unperm], axis=0)
    wpb = wp[...].astype(BF16)

    def merge(i0, count):
        tiles = [taps(x, i0, count, a, half) for x in (x2, x3) for a in range(4)]
        return silu(dot_nt(jnp.concatenate(tiles, axis=1), jnp.concatenate([wma[...], wmb[...]], axis=1))).astype(BF16)

    merged = [merge(t * BM, BM) for t in range(pairs // BM)]
    lines = []
    for t in range(pairs // BM):
        update = dot_nt(wpb, merged[t])
        for b in range(BM):
            u = update[:, b * half : (b + 1) * half]
            for q in range(2):
                line = jnp.concatenate([u[2 * q * COUT : (2 * q + 1) * COUT], u[(2 * q + 1) * COUT : (2 * q + 2) * COUT]], axis=1)
                lines.append(line)
    lines = jnp.concatenate(lines, axis=0)
    high = lines.astype(BF16)
    low = (lines - high.astype(F32)).astype(BF16)
    woven = dot_nn(jnp.concatenate([high, low], axis=1), unperm)
    for h in range(height):
        out_ref[:, h, :] = woven[h * COUT : (h + 1) * COUT] + rest_ref[h * COUT : (h + 1) * COUT]


def shards(latlon, table, k1, k2, kd, kc, ku, km, kp):
    n = lax.axis_size("lon")
    k1, kd = jnp.swapaxes(k1, 2, 3), jnp.swapaxes(kd, 2, 3)
    channels, sub_rows, width = latlon.shape
    height, cols = table.shape[1], table.shape[2]
    vm = pl.BlockSpec(memory_space=pltpu.VMEM)
    groups = height // PER
    sides = 2 * groups * 2 * HALO
    around = jax.ShapeDtypeStruct((cols + 8 * HALO + sides, PER * channels), BF16)
    C, C2, COUT = k1.shape[3], kd.shape[3], kp.shape[0]
    weights = (
        jax.ShapeDtypeStruct((4 * PER * channels, 2 * C * PER), BF16),
        jax.ShapeDtypeStruct((4 * PER * channels, 2 * C), BF16),
        jax.ShapeDtypeStruct((4 * PER * channels, 2 * C), BF16),
        jax.ShapeDtypeStruct((4 * PER * channels, 2 * C), BF16),
        jax.ShapeDtypeStruct((4 * C, 16 * C), BF16),
        jax.ShapeDtypeStruct((12 * C, C2), BF16),
        jax.ShapeDtypeStruct((C2, 9 * C2), BF16),
        jax.ShapeDtypeStruct((4 * C, 4 * C2), BF16),
        jax.ShapeDtypeStruct((4 * C, 16 * C), BF16),
        jax.ShapeDtypeStruct((4 * C, 16 * C), BF16),
        jax.ShapeDtypeStruct((4 * COUT, 4 * C), F32),
    )
    ready = pl.pallas_call(
        functools.partial(exchange_kernel, n),
        out_shape=(jax.ShapeDtypeStruct((groups, cols, PER * channels), BF16), around,
                   jax.ShapeDtypeStruct((height, cols // 2, 2 * C), F32),
                   jax.ShapeDtypeStruct((height * COUT, cols), F32)) + weights,
        in_specs=[pl.BlockSpec(memory_space=pltpu.HBM)] * 9,
        out_specs=(vm,) * 15,
        scratch_shapes=[
            pltpu.VMEM(table.shape, table.dtype),
        ] + [pltpu.VMEM(k.shape, BF16) for k in (k1, k2, kd, kc, ku, km, kp)] + [
            pltpu.VMEM((n, channels, sub_rows, cols), BF16),
            pltpu.VMEM((sides, PER * channels), BF16),
            pltpu.VMEM((height * cols, 2 * cols), BF16),
            pltpu.VMEM((PER * sides, 2 * cols), BF16),
            pltpu.VMEM((PER * sides, PER * channels), jnp.int32),
            pltpu.VMEM((height * cols, PER * channels), jnp.int32),
            pltpu.VMEM((PER * PER * channels, PER * channels), BF16),
            pltpu.SemaphoreType.DMA,
            pltpu.SemaphoreType.DMA,
            pltpu.SemaphoreType.DMA,
            pltpu.SemaphoreType.DMA,
            pltpu.SemaphoreType.DMA,
            pltpu.SemaphoreType.DMA((8,)),
        ],
        compiler_params=pltpu.CompilerParams(collective_id=0, has_side_effects=True, vmem_limit_bytes=32 * 2**20),
        name="exchange",
    )(*(pltpu.with_memory_space_constraint(v, pltpu.HBM) for v in (latlon, table, k1, k2, kd, kc, ku, km, kp)))
    J = cols // 2 + 2 * HALO
    pairs = height // 2
    return pl.pallas_call(
        unet_kernel,
        out_shape=jax.ShapeDtypeStruct((COUT, height, cols), F32),
        in_specs=[vm] * 15,
        out_specs=vm,
        scratch_shapes=[
            pltpu.VMEM((pairs + 5, 2, J, 4 * C), BF16),
            pltpu.VMEM((pairs + 4, 2, J, 4 * C), BF16),
            pltpu.VMEM((pairs + 1, 2, J, 4 * C), BF16),
            pltpu.VMEM((pairs + 5, J, 3 * C2), BF16),
            pltpu.VMEM((pairs + 2, J, 2 * C2), BF16),
        ],
        compiler_params=pltpu.CompilerParams(vmem_limit_bytes=32 * 2**20),
        name="unet",
    )(*ready)


def solution(mesh):
    return jax.shard_map(
        shards,
        mesh=mesh,
        in_specs=(P("groups", "lon", None), P(None, None, "lon")) + (P(),) * 7,
        out_specs=P("groups", None, "lon"),
        check_vma=False,
    )
```

```python
import functools

import jax
import jax.numpy as jnp
from jax import lax
from jax.experimental import pallas as pl
from jax.experimental.pallas import tpu as pltpu
from jax.sharding import PartitionSpec as P

MESH = pl.DeviceIdType.MESH
F32 = jnp.float32
BF16 = jnp.bfloat16
HALO = 4
PER = 8
OFFSETS = (0, 1, 2, -1)
NT = (((1,), (1,)), ((), ()))


def dot_nt(a, b):
    return lax.dot_general(a, b, NT, preferred_element_type=F32)


def silu(x):
    half = 0.5 * x
    return half * jnp.tanh(half) + half


def dot_nn(a, b):
    return jnp.dot(a, b, preferred_element_type=F32)


def clear(*arrays):
    for w in arrays:
        w[...] = jnp.zeros_like(w)


def inner_taps(v):
    half = v.shape[0] // 2
    even, odd = v[:half], v[half:]
    row = lax.broadcasted_iota(jnp.int32, even.shape, 0)
    after = jnp.where(row == half - 1, 0.0, pltpu.roll(even, half - 1, 0))
    before = jnp.where(row == 0, 0.0, pltpu.roll(odd, 1, 0))
    return jnp.concatenate([even, odd, after, before], axis=1).astype(BF16)


def fill(w, kernel, cin, first_in):
    C = kernel.shape[2]
    for q in range(2):
        for p in range(2):
            for a in range(4):
                for l, off in enumerate(OFFSETS):
                    kr, kcol = a - q, off - p + 1
                    if 0 <= kr < 3 and 0 <= kcol < 3:
                        at = (q * 2 + p) * C
                        lane = a * 4 * cin + l * cin
                        w[at : at + C, lane : lane + cin] = kernel[kr, kcol][:, first_in : first_in + cin]


def fine_weights(k1, k2, km, w1, wlast, wfirst, wnext, w2, wma, wmb):
    channels, C = k1.shape[2], k1.shape[3]
    wide = PER * channels
    clear(w1, wlast, wfirst, wnext, w2, wma, wmb)
    for p in range(2):
        for l, off in enumerate(OFFSETS):
            if not 0 <= off - p + 1 < 3:
                continue
            k = [k1[kr, off - p + 1] for kr in range(3)]
            lane = l * wide
            for r in range(PER):
                at = (r * 2 + p) * C
                for kr in range(3):
                    if 0 <= r + kr - 1 < PER:
                        to = lane + (r + kr - 1) * channels
                        w1[to : to + channels, at : at + C] = k[kr]
            end = lane + (PER - 1) * channels
            wlast[end : end + channels, p * C : (p + 1) * C] = k[0]
            wfirst[lane : lane + channels, p * C : (p + 1) * C] = k[0]
            wnext[lane : lane + channels, p * C : (p + 1) * C] = k[2]
    fill(w2, k2, C, 0)
    fill(wma, km, C, 0)
    fill(wmb, km, C, C)


def coarse_weights(kd, kc, ku, kp, wd, wc, wu, wp):
    C, C2 = kd.shape[2], kd.shape[3]
    COUT = kp.shape[0]
    clear(wd, wc, wu, wp)
    for a in range(3):
        for l, kcol in ((0, 1), (1, 2), (3, 0)):
            wd[a * 4 * C + l * C : a * 4 * C + (l + 1) * C] = kd[a, kcol]
        for s, kcol in enumerate((1, 2, 0)):
            wc[:, (a * 3 + s) * C2 : (a * 3 + s + 1) * C2] = kc[a, kcol]
    for q, rows in ((0, ((0, 1),)), (1, ((0, 0), (1, 2)))):
        for p, columns in ((0, ((0, 1),)), (1, ((0, 0), (1, 2)))):
            at = (q * 2 + p) * C
            for ri, kr in rows:
                for ci, kcol in columns:
                    lane = (ri * 2 + ci) * C2
                    wu[at : at + C, lane : lane + C2] = ku[kr, kcol]
    for g in range(4):
        wp[g * COUT : (g + 1) * COUT, g * C : (g + 1) * C] = kp[...].astype(F32)


def exchange_kernel(n, lat_ref, tab_hbm, k1_hbm, k2_hbm, kd_hbm, kc_hbm, ku_hbm, km_hbm, kp_hbm,
                    own_ref, halo_ref, pre_ref, w1, wlast, wfirst, wnext, w2, wd, wc, wu, wma, wmb, wp,
                    tab_ref, k1, k2, kd, kc, ku, km, kp, recv, edge, hot, edge_hot, edge_at, at_ref, fold_ref,
                    send_sem, recv_sem, own_sem, hsend, hrecv, load_sem):
    me = lax.axis_index("lon")
    group = lax.axis_index("groups")
    cols = recv.shape[3]
    height = tab_ref.shape[1]
    per = height // own_ref.shape[0]
    sub_rows = lat_ref.shape[1]
    channels = own_ref.shape[2] // per
    barrier = pltpu.get_barrier_semaphore()

    def greet(d, carry):
        pl.semaphore_signal(barrier, inc=1, device_id=(group, lax.rem(me + d, n)), device_id_type=MESH)
        return carry

    lax.fori_loop(1, n, greet, 0)
    mine = pltpu.make_async_copy(lat_ref.at[:, :, pl.ds(pl.multiple_of(me * cols, cols), cols)], recv.at[me], own_sem)
    mine.start()
    loads = [pltpu.make_async_copy(src, dst, load_sem.at[i]) for i, (src, dst) in enumerate((
        (tab_hbm, tab_ref), (k1_hbm, k1), (k2_hbm, k2), (kd_hbm, kd), (kc_hbm, kc), (ku_hbm, ku), (km_hbm, km), (kp_hbm, kp)))]
    for load in loads:
        load.start()
    pl.semaphore_wait(barrier, n - 1)

    def block_copy(target):
        return pltpu.make_async_remote_copy(
            src_ref=lat_ref.at[:, :, pl.ds(pl.multiple_of(target * cols, cols), cols)],
            dst_ref=recv.at[me],
            send_sem=send_sem,
            recv_sem=recv_sem,
            device_id=(group, target),
            device_id_type=MESH,
        )

    def send(k, carry):
        target = n - 4 - k // 4 * 4 + (me + k + 1) % 4

        @pl.when(target != me)
        def _():
            block_copy(target).start()

        return carry

    lax.fori_loop(0, n, send, 0)

    loads[0].wait()
    p = lax.broadcasted_iota(jnp.int32, (cols, cols), 0)
    w = lax.broadcasted_iota(jnp.int32, (cols, cols), 1)
    half = cols // 2
    perm = (w == jnp.where(p < half, 2 * p, 2 * p - cols + 1)).astype(F32).astype(BF16)
    rows_at = dot_nt(perm, tab_ref[0].astype(F32).astype(BF16)).astype(jnp.int32)
    cols_at = dot_nt(perm, (tab_ref[1] - me * cols).astype(F32).astype(BF16)).astype(jnp.int32)
    wide = per * channels
    lane = lax.broadcasted_iota(jnp.int32, (cols, wide), 1)
    wide_hot = lax.broadcasted_iota(jnp.int32, (cols, 2 * cols), 1)
    held = sub_rows * channels
    per_tile = wide // held
    spot = lane // held * sub_rows + lane % sub_rows
    pair = rows_at // (2 * sub_rows)
    col_key = cols_at + rows_at // sub_rows % 2 * cols
    row_key = pair * sub_rows + rows_at % sub_rows
    groups = own_ref.shape[0]
    strip = 2 * HALO
    ep = lax.broadcasted_iota(jnp.int32, (2 * strip, cols), 0)
    ew = lax.broadcasted_iota(jnp.int32, (2 * strip, cols), 1)
    first = jnp.where(ep < HALO, 2 * ep, 2 * (ep - HALO) + 1)
    last = jnp.where(ep < strip + HALO, 2 * (ep - strip) + 1, 2 * (ep - strip - HALO)) + cols - strip
    edge_perm = (ew == jnp.where(ep < strip, first, last)).astype(F32).astype(BF16)
    edge_rows = dot_nt(edge_perm, tab_ref[0].astype(F32).astype(BF16)).astype(jnp.int32)
    edge_cols = dot_nt(edge_perm, (tab_ref[1] - me * cols).astype(F32).astype(BF16)).astype(jnp.int32)
    edge_col_key = edge_cols + edge_rows // sub_rows % 2 * cols
    edge_row_key = edge_rows // (2 * sub_rows) * sub_rows + edge_rows % sub_rows
    edge_held = 2 * groups * strip

    def edge_of(keys, q, width):
        return jnp.concatenate([jnp.broadcast_to(keys[side * strip : (side + 1) * strip, g * per + q : g * per + q + 1], (strip, width))
                                for side in range(2) for g in range(groups)], axis=0)

    for q in range(per):
        edge_hot[q * edge_held : (q + 1) * edge_held] = (edge_of(edge_col_key, q, 2 * cols) == wide_hot[:edge_held]).astype(F32).astype(BF16)
        edge_at[q * edge_held : (q + 1) * edge_held] = edge_of(edge_row_key, q, wide) - spot[:edge_held]
    for h in range(height):
        hot[h * cols : (h + 1) * cols] = (col_key[:, h : h + 1] == wide_hot).astype(F32).astype(BF16)
        at_ref[h * cols : (h + 1) * cols] = jnp.broadcast_to(row_key[:, h : h + 1], (cols, wide)) - spot
    fi = lax.broadcasted_iota(jnp.int32, (per * wide, wide), 0)
    fo = lax.broadcasted_iota(jnp.int32, (per * wide, wide), 1)
    fold_ref[...] = ((fi // wide == fo // channels) & (fi % held // sub_rows == fo % channels)).astype(F32).astype(BF16)
    for load in loads[1:]:
        load.wait()
    coarse_weights(kd, kc, ku, kp, wd, wc, wu, wp)
    fine_weights(k1, k2, km, w1, wlast, wfirst, wnext, w2, wma, wmb)
    mine.wait()

    blocks = pltpu.make_async_remote_copy(
        src_ref=recv.at[pl.ds(0, n - 1)], dst_ref=recv.at[pl.ds(0, n - 1)], send_sem=send_sem, recv_sem=recv_sem,
        device_id=(group, lax.rem(me + 1, n)), device_id_type=MESH)
    blocks.wait_recv()

    def halo(src, dst, shift):
        return pltpu.make_async_remote_copy(
            src_ref=src, dst_ref=dst, send_sem=hsend, recv_sem=hrecv,
            device_id=(group, lax.rem(me + shift + 2 * n, n)), device_id_type=MESH)

    lead = groups * strip
    firsts, lasts = edge.at[pl.ds(0, lead)], edge.at[pl.ds(lead, lead)]

    def source_of():
        arrived = recv[...].reshape(n // 2, 2, held, cols)
        return jnp.concatenate([arrived[:, 0], arrived[:, 1]], axis=2).reshape(n // 2 * held, 2 * cols)

    tiles = n // 2 * held // wide

    def pick(got, at, q, count):
        one = jnp.zeros((count, wide), F32)
        for t in range(tiles):
            value = got[q * count : (q + 1) * count, t * wide : (t + 1) * wide]
            one = jnp.where(at == t * per_tile * sub_rows, value, one)
        return one.astype(BF16)

    got = dot_nt(edge_hot[...], source_of())
    picked = [pick(got, edge_at[q * edge_held : (q + 1) * edge_held], q, edge_held) for q in range(per)]
    edge[...] = jnp.dot(jnp.concatenate(picked, axis=1), fold_ref[...], preferred_element_type=F32).astype(BF16)
    for src, first_row, count, shift in (
        (lasts, cols + 4 * strip, lead, 1), (firsts, cols + 4 * strip + lead, lead, -1),
        (edge.at[pl.ds(lead, 2 * strip)], cols, 2 * strip, n // 2 + 1), (edge.at[pl.ds(0, 2 * strip)], cols + 2 * strip, 2 * strip, n // 2 - 1),
    ):
        halo(src, halo_ref.at[pl.ds(first_row, count)], shift).start()

    @pl.when(me >= 0)
    def _():
        source = source_of()
        for g in range(groups):
            got = dot_nt(hot[g * per * cols : (g + 1) * per * cols], source)
            picked = [pick(got, at_ref[(g * per + q) * cols : (g * per + q + 1) * cols], q, cols) for q in range(per)]
            own_ref[g] = jnp.dot(jnp.concatenate(picked, axis=1), fold_ref[...], preferred_element_type=F32).astype(BF16)
            if g == 0:
                halo(own_ref.at[0], halo_ref.at[pl.ds(0, cols)], n // 2).start()

    middle = jnp.concatenate([inner_taps(own_ref[g].astype(F32)) for g in range(groups)], axis=0)
    half, pair = cols // 2, 2 * k1.shape[3]
    base = dot_nn(middle, w1[...])
    above = dot_nn(middle[: (groups - 1) * half], wlast[...])
    below = dot_nn(middle[half:], wnext[...])
    for g in range(groups):
        for r in range(per):
            v = base[g * half : (g + 1) * half, r * pair : (r + 1) * pair]
            if r == 0 and g > 0:
                v = v + above[(g - 1) * half : g * half]
            if r == per - 1 and g < groups - 1:
                v = v + below[g * half : (g + 1) * half]
            if g + r > 0:
                v = jnp.concatenate([v[:strip], silu(v[strip : half - strip]), v[half - strip :]], axis=0)
            pre_ref[g * per + r] = v
    blocks.wait_send()
    every = halo(halo_ref, halo_ref, 1)
    every.wait_send()
    every.wait_recv()


def unet_kernel(own_ref, halo_ref, pre_ref, w1, wlast, wfirst, wnext, w2, wd, wc, wu, wma, wmb, wp, out_ref, x1, x2, x3, xc, xu):
    groups, cols, wide = own_ref.shape
    height = groups * PER
    channels = wide // PER
    half = cols // 2
    J = half + 2 * HALO
    C = w2.shape[0] // 4
    C2 = wd.shape[1]
    COUT = wp.shape[0] // 4
    pairs = height // 2
    AB = pairs + 1

    strip = 2 * HALO
    upper = lax.broadcasted_iota(jnp.int32, (strip, wide), 0) < HALO

    def spread(g, l, r):
        even = jnp.concatenate([g[:half], jnp.where(upper, r, l)], axis=0)
        odd = jnp.concatenate([g[half:], pltpu.roll(jnp.where(upper, l, r), HALO, 0)], axis=0)
        return jnp.concatenate([even, odd, pltpu.roll(even, J - 1, 0), pltpu.roll(odd, 1, 0)], axis=1).astype(BF16)

    around = halo_ref[...].astype(F32)
    corners, sides = around[cols : cols + 4 * strip], around[cols + 4 * strip :]
    row = lax.broadcasted_iota(jnp.int32, (strip, wide), 0)
    none = jnp.zeros((strip, wide), F32)

    def rim(g, l, r):
        even, odd = jnp.where(upper, r, l), pltpu.roll(jnp.where(upper, l, r), HALO, 0)
        after = jnp.where(row == strip - 1, g[0:1], pltpu.roll(even, strip - 1, 0))
        before = jnp.where(row == 0, g[cols - 1 : cols], pltpu.roll(odd, 1, 0))
        ring = jnp.concatenate([even, odd, after, before], axis=1)
        ends = jnp.concatenate([none, none, jnp.where(row == 0, even, 0.0), jnp.where(row == strip - 1, odd, 0.0)], axis=1)
        return jnp.concatenate([ring, ends], axis=0).astype(BF16)

    own = [own_ref[g].astype(F32) for g in range(groups)]
    lefts = [sides[g * strip : (g + 1) * strip] for g in range(groups)]
    rights = [sides[(groups + g) * strip : (groups + g + 1) * strip] for g in range(groups)]
    rims = jnp.concatenate([rim(own[g], lefts[g], rights[g]) for g in range(groups)], axis=0)
    top = spread(own[0], lefts[0], rights[0])
    across = spread(around[:cols], corners[:strip], corners[2 * strip : 3 * strip])

    def neighbours(v):
        count = v.shape[0]
        v = v.reshape(count // J, J, v.shape[1])
        lane = lax.broadcasted_iota(jnp.int32, v.shape, 2)
        other = jnp.where(lane < C, pltpu.roll(v, J - 1, 1), pltpu.roll(v, 1, 1))
        return jnp.concatenate([v, other], axis=2).astype(BF16)

    def store_pair(x, i0, count, s):
        x[pl.ds(i0, count), 1] = neighbours(s[:, : 2 * C])
        x[pl.ds(i0 + 1, count), 0] = neighbours(s[:, 2 * C :])

    def wrap(x):
        x[0, 0] = x[AB, 1]
        x[AB, 0] = x[0, 1]
        x[AB - 1, 1] = jnp.zeros(x.shape[2:], BF16)

    def taps(x, i0, count, a, width):
        v = x[pl.ds(i0 + a // 2, count), a % 2, 0:width]
        return v.reshape(count * width, v.shape[-1])

    B = 8
    BM = 4

    def own_loop(steps, body):
        for t in range(steps):
            body(t)

    R = 2 * strip
    base = dot_nn(rims, w1[...])
    above = dot_nn(rims[: (groups - 1) * R], wlast[...])
    below = dot_nn(rims[R:], wnext[...])
    own_top = dot_nn(across, wfirst[...])
    anti_top = dot_nn(top, wfirst[...])
    anti = dot_nn(across, w1[...])
    for g in range(groups):
        for r in range(PER):
            e = base[g * R : (g + 1) * R, r * 2 * C : (r + 1) * 2 * C]
            if r == 0 and g > 0:
                e = e + above[(g - 1) * R : g * R]
            if r == PER - 1 and g < groups - 1:
                e = e + below[g * R : (g + 1) * R]
            ring, ends = e[:strip], e[strip:]
            v = pre_ref[g * PER + r]
            head = v[:strip] + jnp.where(row == 0, pltpu.roll(ends, 1, 0), 0.0)
            tail = v[half - strip :] + jnp.where(row == strip - 1, pltpu.roll(ends, strip - 1, 0), 0.0)
            inner = v[strip : half - strip]
            if g + r > 0:
                v = silu(jnp.concatenate([head, tail, ring], axis=0))
                v = jnp.concatenate([v[:strip], inner, v[strip:]], axis=0)
            else:
                v = silu(jnp.concatenate([head, inner, tail, ring], axis=0) + own_top)
            slot = g * PER + r + 1
            x1[slot // 2, slot % 2] = neighbours(v)[0]
    for r in range(PER):
        slot = groups * PER + r + 3
        if slot // 2 < x1.shape[0]:
            v = anti[:, r * 2 * C : (r + 1) * 2 * C]
            x1[slot // 2, slot % 2] = neighbours(silu(v + anti_top if r == 0 else v))[0]
    wrap(x1)

    def second(i0, count):
        acc = dot_nt(jnp.concatenate([taps(x1, i0, count, a, J) for a in range(4)], axis=1), w2[...])
        store_pair(x2, i0, count, silu(acc))

    second(AB, 2)
    own_loop(pairs // B, lambda t: second(t * B, B))
    wrap(x2)

    def shifts(v, both):
        v = v.reshape(v.shape[0] // J, J, v.shape[1])
        parts = [v, pltpu.roll(v, J - 1, 1)]
        if both:
            parts.append(pltpu.roll(v, 1, 1))
        return jnp.concatenate(parts, axis=2).astype(BF16)

    def down(i0, slot, count):
        acc = dot_nn(jnp.concatenate([taps(x2, i0, count, a, J) for a in range(3)], axis=1), wd[...])
        xc[pl.ds(slot, count)] = shifts(silu(acc), True)

    own_loop(pairs // B, lambda t: down(t * B, t * B + 1, B))
    down(AB, pairs + 3, 2)
    xc[0] = xc[pairs + 3]
    xc[pairs + 2] = xc[1]
    xc[pairs + 1] = jnp.zeros(xc.shape[1:], BF16)

    def coarse(i0, slot, count):
        acc = dot_nt(jnp.concatenate([xc[pl.ds(i0 + a, count)].reshape(count * J, 3 * C2) for a in range(3)], axis=1), wc[...])
        xu[pl.ds(slot, count)] = shifts(silu(acc), False)

    own_loop(pairs // B, lambda t: coarse(t * B, t * B, B))
    coarse(pairs + 2, pairs + 1, 1)
    xu[pairs] = jnp.zeros(xu.shape[1:], BF16)

    def up(i0, count):
        return silu(dot_nt(jnp.concatenate([xu[pl.ds(i0 + a, count)].reshape(count * J, 2 * C2) for a in range(2)], axis=1), wu[...]))

    def up_own(t):
        store_pair(x3, t * B, B, up(t * B, B))

    own_loop(pairs // B, up_own)
    v = xu[pairs + 1]
    x3[0, 0] = neighbours(silu(dot_nt(v, wu[0 : 2 * C, : 2 * C2])))[0]
    x3[AB - 1, 1] = jnp.zeros(x3.shape[2:], BF16)

    p = lax.broadcasted_iota(jnp.int32, (cols, cols), 0)
    w = lax.broadcasted_iota(jnp.int32, (cols, cols), 1)
    unperm = (w == jnp.where(p < half, 2 * p, 2 * p - cols + 1)).astype(F32).astype(BF16)
    unperm = jnp.concatenate([unperm, unperm], axis=0)
    wpb = wp[...].astype(BF16)
    plain = [own_ref[g].astype(F32).T for g in range(groups)]

    def merge(i0, count):
        tiles = [taps(x, i0, count, a, half) for x in (x2, x3) for a in range(4)]
        return silu(dot_nt(jnp.concatenate(tiles, axis=1), jnp.concatenate([wma[...], wmb[...]], axis=1))).astype(BF16)

    merged = [merge(t * BM, BM) for t in range(pairs // BM)]
    lines = []
    for t in range(pairs // BM):
        update = dot_nt(wpb, merged[t])
        for b in range(BM):
            u = update[:, b * half : (b + 1) * half]
            for q in range(2):
                line = jnp.concatenate([u[2 * q * COUT : (2 * q + 1) * COUT], u[(2 * q + 1) * COUT : (2 * q + 2) * COUT]], axis=1)
                h = 2 * (t * BM + b) + q
                at = (h % PER) * channels
                lines.append(line + plain[h // PER][at : at + COUT])
    lines = jnp.concatenate(lines, axis=0)
    high = lines.astype(BF16)
    low = (lines - high.astype(F32)).astype(BF16)
    woven = dot_nn(jnp.concatenate([high, low], axis=1), unperm)
    for h in range(height):
        out_ref[:, h, :] = woven[h * COUT : (h + 1) * COUT]


def shards(latlon, table, k1, k2, kd, kc, ku, km, kp):
    n = lax.axis_size("lon")
    k1, kd = jnp.swapaxes(k1, 2, 3), jnp.swapaxes(kd, 2, 3)
    channels, sub_rows, width = latlon.shape
    height, cols = table.shape[1], table.shape[2]
    vm = pl.BlockSpec(memory_space=pltpu.VMEM)
    groups = height // PER
    sides = 2 * groups * 2 * HALO
    around = jax.ShapeDtypeStruct((cols + 8 * HALO + sides, PER * channels), BF16)
    C, C2, COUT = k1.shape[3], kd.shape[3], kp.shape[0]
    weights = (
        jax.ShapeDtypeStruct((4 * PER * channels, 2 * C * PER), BF16),
        jax.ShapeDtypeStruct((4 * PER * channels, 2 * C), BF16),
        jax.ShapeDtypeStruct((4 * PER * channels, 2 * C), BF16),
        jax.ShapeDtypeStruct((4 * PER * channels, 2 * C), BF16),
        jax.ShapeDtypeStruct((4 * C, 16 * C), BF16),
        jax.ShapeDtypeStruct((12 * C, C2), BF16),
        jax.ShapeDtypeStruct((C2, 9 * C2), BF16),
        jax.ShapeDtypeStruct((4 * C, 4 * C2), BF16),
        jax.ShapeDtypeStruct((4 * C, 16 * C), BF16),
        jax.ShapeDtypeStruct((4 * C, 16 * C), BF16),
        jax.ShapeDtypeStruct((4 * COUT, 4 * C), F32),
    )
    ready = pl.pallas_call(
        functools.partial(exchange_kernel, n),
        out_shape=(jax.ShapeDtypeStruct((groups, cols, PER * channels), BF16), around,
                   jax.ShapeDtypeStruct((height, cols // 2, 2 * C), F32)) + weights,
        in_specs=[pl.BlockSpec(memory_space=pltpu.HBM)] * 9,
        out_specs=(vm,) * 14,
        scratch_shapes=[
            pltpu.VMEM(table.shape, table.dtype),
        ] + [pltpu.VMEM(k.shape, BF16) for k in (k1, k2, kd, kc, ku, km, kp)] + [
            pltpu.VMEM((n, channels, sub_rows, cols), BF16),
            pltpu.VMEM((sides, PER * channels), BF16),
            pltpu.VMEM((height * cols, 2 * cols), BF16),
            pltpu.VMEM((PER * sides, 2 * cols), BF16),
            pltpu.VMEM((PER * sides, PER * channels), jnp.int32),
            pltpu.VMEM((height * cols, PER * channels), jnp.int32),
            pltpu.VMEM((PER * PER * channels, PER * channels), BF16),
            pltpu.SemaphoreType.DMA,
            pltpu.SemaphoreType.DMA,
            pltpu.SemaphoreType.DMA,
            pltpu.SemaphoreType.DMA,
            pltpu.SemaphoreType.DMA,
            pltpu.SemaphoreType.DMA((8,)),
        ],
        compiler_params=pltpu.CompilerParams(collective_id=0, has_side_effects=True, vmem_limit_bytes=32 * 2**20),
        name="exchange",
    )(*(pltpu.with_memory_space_constraint(v, pltpu.HBM) for v in (latlon, table, k1, k2, kd, kc, ku, km, kp)))
    J = cols // 2 + 2 * HALO
    pairs = height // 2
    return pl.pallas_call(
        unet_kernel,
        out_shape=jax.ShapeDtypeStruct((COUT, height, cols), F32),
        in_specs=[vm] * 14,
        out_specs=vm,
        scratch_shapes=[
            pltpu.VMEM((pairs + 5, 2, J, 4 * C), BF16),
            pltpu.VMEM((pairs + 4, 2, J, 4 * C), BF16),
            pltpu.VMEM((pairs + 1, 2, J, 4 * C), BF16),
            pltpu.VMEM((pairs + 5, J, 3 * C2), BF16),
            pltpu.VMEM((pairs + 2, J, 2 * C2), BF16),
        ],
        compiler_params=pltpu.CompilerParams(vmem_limit_bytes=32 * 2**20),
        name="unet",
    )(*ready)


def solution(mesh):
    return jax.shard_map(
        shards,
        mesh=mesh,
        in_specs=(P("groups", "lon", None), P(None, None, "lon")) + (P(),) * 7,
        out_specs=P("groups", None, "lon"),
        check_vma=False,
    )
```
